32 devices in a mesh: groups: 2 (over y), row: 8 (over z, x), col: 2 (over core).
Axes of the slice: x: 2, y: 2, z: 4, core: 2. Of those that a mesh axis runs over, the one named last changes fastest.
Arguments:
- tokens: bfloat16 [768, 6144], P(('groups', 'col'), 'row'), parts along dimension 0, may hold values from -6 to 6
- cotangent: bfloat16 [768, 6144], P(('groups', 'col'), 'row'), parts along dimension 0, may hold values from -6 to 6
- up_weight: bfloat16 [6144, 24576], P('col', 'row'), may hold values from -0.109375 to 0.109375
- up_bias: float32 [24576], P('row'), may hold values from -3 to 3
- down_weight: bfloat16 [24576, 6144], P('row', 'col'), may hold values from -0.0546875 to 0.0546875
- norm_gain: float32 [6144], replicated, may hold values from 0.25 to 1.75
Outputs:
- block_out: bfloat16 [768, 6144], P(('groups', 'col'), 'row'), parts along dimension 0
- grad_x: bfloat16 [768, 6144], P(('groups', 'col'), 'row'), parts along dimension 0
- grad_in: bfloat16 [12288, 24576], P(('groups', 'col'), 'row'), parts along dimension 0
- grad_out: bfloat16 [49152, 6144], P(('groups', 'row'), 'col'), parts along dimension 0
- grad_bias: float32 [49152], P(('groups', 'row')), parts along dimension 0
- grad_gain: float32 [12288], P(('groups', 'row')), parts along dimension 0
The draws below stay inside these ranges and needn't reach their ends.
There are 2 independent parts, one for each index of `groups`. The reference program is written for one: setup_inputs(seed, part) draws one part's arguments, and reference() takes and returns one part's arrays. A program takes and returns all parts, laid end to end along the dimension named above; an argument that names none is the same for every part. Nothing has to cross between parts.
All inputs are finite; a program needn't handle non-finite values.
Results may differ from the reference program's by a relative error of at most 0.0075.
Values may be sent and summed in bfloat16 or wider, within the bound.
No kernel may reach another device: no remote copies, remote signals or barrier semaphores. Data moves between devices by JAX's collectives and lax.ppermute only.
A program may use at most 320 MiB of HBM per device.

```python
import jax
import jax.numpy as jnp
from jax import lax

D = 6144
FF = 24576
TOK_COL = 192
TOKENS = 384
N_COL = 2


def strengthened(result, rng, source, target, blocks, factor):
    owner, partner = [(jnp.arange(result.shape[position]) // (result.shape[position] // blocks)).reshape([-1 if axis == position else 1 for axis in range(result.ndim)]) for position in (source, target)]
    chosen = jax.random.permutation(rng, blocks)[partner]
    strong = (owner == chosen) | (owner == (partner + blocks // 2) % blocks)
    return jnp.where(strong, factor * result, result)


def levels(key, dims, pieces, least, high):
    factor_of, own = 1.0, jax.random.fold_in(key, 6)
    for axis_at, parts in pieces:
        steps = jnp.exp(jax.random.uniform(jax.random.fold_in(own, axis_at), (parts,), jnp.float32, least / len(pieces), high / len(pieces)))
        factor_of = factor_of * jnp.repeat(steps, dims[axis_at] // parts).reshape([-1 if axis == axis_at else 1 for axis in range(len(dims))])
    return factor_of


def bell_draw(own_key, extent, deviation, most, split=(), held_as=jnp.bfloat16):
    array = jax.random.normal(own_key, extent, jnp.float32) * deviation
    if len(split) > 0:
        array = levels(own_key, extent, split, -0.22, 0.18) * array
    return jnp.clip(array, min=-most, max=most).astype(held_as)


def gaussian_with(own_key, dims, deviation, reach, cuts, heavy, dtype=jnp.bfloat16):
    array = deviation * jax.random.normal(own_key, dims, jnp.float32)
    if cuts:
        array = array * levels(own_key, dims, cuts, -0.22, 0.18)
    return jnp.clip(strengthened(array, jax.random.fold_in(own_key, 3), *heavy), -reach, reach).astype(dtype)


def setup_inputs(seed: int = 0, part: int = 0) -> dict:
    key_of = jax.random.split(jax.random.key(seed), 7)
    part_keys = jax.random.split(jax.random.fold_in(key_of[6], part), 7)
    tokens = bell_draw(part_keys[0], (TOKENS, D), 1.0, 6.0, ((0, 2), (1, 8)))
    cotangent = bell_draw(part_keys[1], (TOKENS, D), 1.0, 6.0, ((0, 2), (1, 8)))
    up_weight = gaussian_with(key_of[2], (D, FF), D ** -0.5, 0.109375, ((0, 2), (1, 8)), (1, 0, 8, 2.0))
    up_bias = bell_draw(key_of[3], (FF,), 0.5, 3.0, ((0, 8),), jnp.float32)
    down_weight = gaussian_with(key_of[4], (FF, D), FF ** -0.5, 0.0546875, ((0, 8), (1, 2)), (0, 1, 8, 2.0))
    norm_gain = jnp.clip(1.0 + 0.15 * jax.random.normal(key_of[5], (D,), jnp.float32), 0.25, 1.75)
    return dict(tokens=tokens, cotangent=cotangent, up_weight=up_weight, up_bias=up_bias, down_weight=down_weight, norm_gain=norm_gain)


norm_eps = 1e-06
root_half = 0.7071067811865476
pdf_scale = 0.3989422804014327

def gelu_parts(hidden):
    cumulative = 0.5 * (1.0 + lax.erf(hidden * root_half))
    density = jnp.exp(-0.5 * hidden * hidden) * pdf_scale
    return (hidden * cumulative, cumulative + hidden * density)

def contract(left, right, left_dim, right_dim):
    return lax.dot_general(left, right, (((left_dim,), (right_dim,)), ((), ())), preferred_element_type=jnp.float32)

def block_grad(left, right):
    total = jnp.zeros((left.shape[1], right.shape[1]), jnp.float32)
    for block in range(N_COL):
        start = block * TOK_COL
        piece = contract(left[start:start + TOK_COL], right[start:start + TOK_COL], 0, 0).astype(jnp.bfloat16)
        piece = lax.optimization_barrier(piece)
        total = total + piece.astype(jnp.float32)
    return total.astype(jnp.bfloat16)

def reference(tokens, cotangent, up_weight, up_bias, down_weight, norm_gain):
    as_float = tokens.astype(jnp.float32)
    token_mean = lax.optimization_barrier(jnp.mean(as_float, axis=1, keepdims=True))
    centered = as_float - token_mean
    inverse_std = lax.rsqrt(lax.optimization_barrier(jnp.mean(centered * centered, axis=1, keepdims=True)) + norm_eps)
    whitened = centered * inverse_std
    normed = (whitened * norm_gain).astype(jnp.bfloat16)
    hidden = jnp.dot(normed, up_weight, preferred_element_type=jnp.float32) + up_bias
    gelu_value, gelu_slope = gelu_parts(hidden)
    activation = gelu_value.astype(jnp.bfloat16)
    block_out = (as_float + jnp.dot(activation, down_weight, preferred_element_type=jnp.float32)).astype(jnp.bfloat16)
    act_grad = contract(cotangent, down_weight, 1, 1)
    hidden_grad = (act_grad * gelu_slope).astype(jnp.bfloat16)
    grad_out = block_grad(activation, cotangent)
    grad_in = block_grad(normed, hidden_grad)
    grad_bias = lax.optimization_barrier(jnp.sum(hidden_grad.astype(jnp.float32), axis=0))
    normed_grad = contract(hidden_grad, up_weight, 1, 1)
    scaled = normed_grad * norm_gain
    first_stat = lax.optimization_barrier(jnp.mean(scaled, axis=1, keepdims=True))
    second_stat = lax.optimization_barrier(jnp.mean(scaled * whitened, axis=1, keepdims=True))
    grad_gain = lax.optimization_barrier(jnp.sum(normed_grad * whitened, axis=0))
    grad_x = (cotangent.astype(jnp.float32) + inverse_std * (scaled - first_stat - whitened * second_stat)).astype(jnp.bfloat16)
    return (block_out, grad_x, grad_in, grad_out, grad_bias, grad_gain)
```

```python
import jax
import jax.numpy as jnp
from jax import lax
from jax.sharding import PartitionSpec as P

norm_eps = 1e-06
root_half = 0.7071067811865476
pdf_scale = 0.3989422804014327
bf16 = jnp.bfloat16
f32 = jnp.float32
ring_limit = 8


def gelu_parts(hidden):
    cumulative = 0.5 * (1.0 + lax.erf(hidden * root_half))
    density = jnp.exp(-0.5 * hidden * hidden) * pdf_scale
    return (hidden * cumulative, cumulative + hidden * density)


def contract(left, right, left_dim, right_dim):
    return lax.dot_general(
        left, right, (((left_dim,), (right_dim,)), ((), ())), preferred_element_type=f32
    )


class Ring:
    def __init__(self, n):
        self.n = n
        self.order = list(range(0, n, 2)) + list(range(n - 1, 0, -2))
        row = lax.axis_index("row")
        half = row // 2
        self.place = jnp.where(row % 2 == 0, half, n - 1 - half)

    def shift(self, x, step):
        n, order = self.n, self.order
        return lax.ppermute(x, "row", [(order[i], order[(i + step) % n]) for i in range(n)])

    def row_at(self, offset):
        n = self.n
        place = (self.place + offset) % n
        return jnp.where(place < n // 2, 2 * place, 2 * (n - 1 - place) + 1)

    def every(self, x):
        n = self.n
        if n > ring_limit:
            return lax.all_gather(x, "row")
        sent = [lax.ppermute(x, "row", [(i, (i + k) % n) for i in range(n)]) for k in range(1, n)]
        return jnp.stack([x] + sent)

    def total(self, x):
        step = 1
        while step < self.n:
            x = x + lax.ppermute(x, "row", [(i, i ^ step) for i in range(self.n)])
            step *= 2
        return x

    def gather(self, x):
        n = self.n
        if n > ring_limit:
            rows = lax.all_gather(x, "row")
            return [lax.dynamic_index_in_dim(rows, self.row_at(k), 0, keepdims=False) for k in range(n)]
        blocks = [None] * n
        blocks[0] = up = down = x
        for k in range(1, n // 2):
            up, down = self.shift(up, -1), self.shift(down, 1)
            blocks[k], blocks[n - k] = up, down
        cut = x.shape[0] // 2
        blocks[n // 2] = jnp.concatenate([self.shift(up[:cut], -1), self.shift(down[cut:], 1)], axis=0)
        return blocks

    def scatter_sum(self, blocks):
        n = self.n
        if n > ring_limit:
            stacked = jnp.stack(blocks)
            offsets = [(self.order.index(r) - self.place) % n for r in range(n)]
            by_row = jnp.stack([lax.dynamic_index_in_dim(stacked, k, 0, keepdims=False) for k in offsets])
            return lax.psum_scatter(by_row.astype(f32), "row", scatter_dimension=0)
        mid = n // 2
        cut = blocks[0].shape[0] // 2
        ahead = self.shift(blocks[mid][:cut], 1)
        back = self.shift(blocks[mid][cut:], -1)
        for k in range(mid - 1, 0, -1):
            to, fro = blocks[k], blocks[n - k]
            if k == mid - 1:
                ahead = jnp.concatenate([(to[:cut].astype(f32) + ahead.astype(f32)).astype(bf16), to[cut:]], axis=0)
                back = jnp.concatenate([fro[:cut], (fro[cut:].astype(f32) + back.astype(f32)).astype(bf16)], axis=0)
            else:
                ahead = (to.astype(f32) + ahead.astype(f32)).astype(bf16)
                back = (fro.astype(f32) + back.astype(f32)).astype(bf16)
            ahead, back = self.shift(ahead, 1), self.shift(back, -1)
        return blocks[0].astype(f32) + ahead.astype(f32) + back.astype(f32)


def swap(x):
    return lax.ppermute(x, "col", [(0, 1), (1, 0)])


def turned(x):
    half = x.shape[0] // 2
    return jnp.concatenate([x[half:], x[:half]], axis=0)


def local(tokens, cotangent, up_weight, up_bias, down_weight, norm_gain):
    tok_count, shard_width = tokens.shape
    n = lax.axis_size("row")
    model_width = n * shard_width
    half_width = model_width // 2
    core = lax.axis_index("col")
    row = lax.axis_index("row")
    ring = Ring(n)
    pairs = n // 2
    first_row = core * pairs

    rows_near = [ring.row_at(j) for j in range(pairs)]
    rows_far = [ring.row_at(j + pairs) for j in range(pairs)]
    near = [(r // pairs) == core for r in rows_near]
    slot = [jnp.where(s, a, b) - first_row for s, a, b in zip(near, rows_near, rows_far)]

    as_float = tokens.astype(f32)
    shard_mean = jnp.mean(as_float, axis=1)
    shard_dev = jnp.sum((as_float - shard_mean[:, None]) ** 2, axis=1)
    own_stats = jnp.stack([shard_mean, shard_dev])
    stats = ring.every(own_stats)
    token_mean = jnp.mean(stats[:, 0], axis=0)
    spread = jnp.sum(stats[:, 1], axis=0) + shard_width * jnp.sum((stats[:, 0] - token_mean) ** 2, axis=0)
    inverse_std = lax.rsqrt(spread / model_width + norm_eps)[:, None]
    whitened = (as_float - token_mean[:, None]) * inverse_std
    gain_local = lax.dynamic_slice_in_dim(norm_gain, row * shard_width, shard_width, 0)
    gain_half = lax.dynamic_slice_in_dim(norm_gain, core * half_width, half_width, 0)
    normed = (whitened * gain_local).astype(bf16)

    def halves(x):
        blocks = ring.gather(x)
        out = jnp.zeros((2 * tok_count, half_width), x.dtype)
        for j in range(pairs):
            keep = jnp.where(near[j], blocks[j], blocks[j + pairs])
            send = jnp.where(near[j], blocks[j + pairs], blocks[j])
            both = jnp.concatenate([keep, swap(send)], axis=0)
            out = lax.dynamic_update_slice(out, both, (0, slot[j] * shard_width))
        return out

    normed_cols = halves(normed)
    cot_cols = halves(cotangent)

    width = up_weight.shape[1]
    mine, theirs = core * (width // 2), (1 - core) * (width // 2)

    def summed(part):
        give = lax.dynamic_slice_in_dim(part, theirs, width // 2, 1)
        own = lax.dynamic_slice_in_dim(part, mine, width // 2, 1)
        return own + swap(turned(give))

    def joined(own):
        other = swap(turned(own))
        return jnp.where(
            core == 0,
            jnp.concatenate([own, other], axis=1),
            jnp.concatenate([other, own], axis=1),
        )

    hidden = summed(jnp.dot(normed_cols, up_weight, preferred_element_type=f32))
    hidden = hidden + lax.dynamic_slice_in_dim(up_bias, mine, width // 2, 0)
    act_grad = summed(contract(cot_cols, down_weight, 1, 1))
    gelu_value, gelu_slope = gelu_parts(hidden)
    activation = joined(gelu_value.astype(bf16))
    hidden_grad = joined((act_grad * gelu_slope).astype(bf16))

    def scattered(part):
        keep, recv = part[:tok_count], swap(part[tok_count:])
        blocks = [None] * n
        for j in range(pairs):
            a = lax.dynamic_slice_in_dim(keep, slot[j] * shard_width, shard_width, 1)
            other_slot = jnp.where(near[j], rows_far[j], rows_near[j]) - (1 - core) * pairs
            b = lax.dynamic_slice_in_dim(recv, other_slot * shard_width, shard_width, 1)
            blocks[j] = jnp.where(near[j], a, b)
            blocks[j + pairs] = jnp.where(near[j], b, a)
        return ring.scatter_sum(blocks)

    branch = scattered(jnp.dot(activation, down_weight, preferred_element_type=f32).astype(bf16))
    block_out = (as_float + branch).astype(bf16)

    normed_half = contract(hidden_grad, up_weight, 1, 1)
    product = normed_half * normed_cols.astype(f32)
    first_part = jnp.sum(normed_half * gain_half, axis=1)
    second_part = jnp.sum(product, axis=1)
    gain_part = jnp.sum(product, axis=0)
    by_token = jnp.stack([first_part, second_part]).reshape(2, 2, tok_count)
    by_token = jnp.where(core == 0, by_token, by_token[:, ::-1])
    gain_full = lax.dynamic_update_slice(jnp.zeros((model_width,), f32), gain_part, (core * half_width,))
    small = jnp.concatenate([by_token.reshape(-1), gain_full])
    small = ring.total(small + swap(small))
    by_token = small[: 4 * tok_count].reshape(2, 2, tok_count)
    by_token = lax.dynamic_index_in_dim(by_token, core, 1, keepdims=False) / model_width
    grad_gain = lax.dynamic_slice_in_dim(small, 4 * tok_count + row * shard_width, shard_width, 0) / gain_local

    normed_grad = scattered(normed_half.astype(bf16))
    grad_out = contract(activation, cot_cols, 0, 0).astype(bf16)
    grad_in = contract(normed_cols, hidden_grad, 0, 0).astype(bf16)
    grad_bias = jnp.sum(hidden_grad.astype(f32), axis=0)
    scaled = normed_grad * gain_local
    grad_x = (
        cotangent.astype(f32)
        + inverse_std * (scaled - by_token[0][:, None] - whitened * by_token[1][:, None])
    ).astype(bf16)
    return (block_out, grad_x, grad_in, grad_out, grad_bias, grad_gain)


def solution(mesh):
    return jax.shard_map(
        local,
        mesh=mesh,
        in_specs=(
            P(("groups", "col"), "row"),
            P(("groups", "col"), "row"),
            P("col", "row"),
            P("row"),
            P("row", "col"),
            P(),
        ),
        out_specs=(
            P(("groups", "col"), "row"),
            P(("groups", "col"), "row"),
            P(("groups", "col"), "row"),
            P(("groups", "row"), "col"),
            P(("groups", "row")),
            P(("groups", "row")),
        ),
        check_vma=False,
    )
```

```python
import jax
import jax.numpy as jnp
from jax import lax
from jax.experimental import pallas as pl
from jax.experimental.pallas import tpu as pltpu
from jax.sharding import PartitionSpec as P

norm_eps = 1e-06
root_half = 0.7071067811865476
pdf_scale = 0.3989422804014327
bf16 = jnp.bfloat16
f32 = jnp.float32
ring_limit = 8


def gelu_parts(hidden):
    cumulative = 0.5 * (1.0 + lax.erf(hidden * root_half))
    density = jnp.exp(-0.5 * hidden * hidden) * pdf_scale
    return (hidden * cumulative, cumulative + hidden * density)


def contract(left, right, left_dim, right_dim):
    return lax.dot_general(
        left, right, (((left_dim,), (right_dim,)), ((), ())), preferred_element_type=f32
    )


class Ring:
    def __init__(self, n):
        self.n = n
        self.order = list(range(0, n, 2)) + list(range(n - 1, 0, -2))
        row = lax.axis_index("row")
        half = row // 2
        self.place = jnp.where(row % 2 == 0, half, n - 1 - half)

    def shift(self, x, step):
        n, order = self.n, self.order
        return lax.ppermute(x, "row", [(order[i], order[(i + step) % n]) for i in range(n)])

    def row_at(self, offset):
        n = self.n
        place = (self.place + offset) % n
        return jnp.where(place < n // 2, 2 * place, 2 * (n - 1 - place) + 1)

    def every(self, x):
        n = self.n
        if n > ring_limit:
            return lax.all_gather(x, "row")
        sent = [lax.ppermute(x, "row", [(i, (i + k) % n) for i in range(n)]) for k in range(1, n)]
        return jnp.stack([x] + sent)

    def total(self, x):
        step = 1
        while step < self.n:
            x = x + lax.ppermute(x, "row", [(i, i ^ step) for i in range(self.n)])
            step *= 2
        return x

    def gather(self, x):
        n = self.n
        if n > ring_limit:
            rows = lax.all_gather(x, "row")
            return [lax.dynamic_index_in_dim(rows, self.row_at(k), 0, keepdims=False) for k in range(n)]
        blocks = [None] * n
        blocks[0] = up = down = x
        for k in range(1, n // 2):
            up, down = self.shift(up, -1), self.shift(down, 1)
            blocks[k], blocks[n - k] = up, down
        cut = x.shape[0] // 2
        blocks[n // 2] = jnp.concatenate([self.shift(up[:cut], -1), self.shift(down[cut:], 1)], axis=0)
        return blocks

    def scatter_sum(self, blocks):
        n = self.n
        if n > ring_limit:
            stacked = jnp.stack(blocks)
            offsets = [(self.order.index(r) - self.place) % n for r in range(n)]
            by_row = jnp.stack([lax.dynamic_index_in_dim(stacked, k, 0, keepdims=False) for k in offsets])
            return lax.psum_scatter(by_row.astype(f32), "row", scatter_dimension=0)
        mid = n // 2
        cut = blocks[0].shape[0] // 2
        ahead = self.shift(blocks[mid][:cut], 1)
        back = self.shift(blocks[mid][cut:], -1)
        for k in range(mid - 1, 0, -1):
            to, fro = blocks[k], blocks[n - k]
            if k == mid - 1:
                ahead = jnp.concatenate([(to[:cut].astype(f32) + ahead.astype(f32)).astype(bf16), to[cut:]], axis=0)
                back = jnp.concatenate([fro[:cut], (fro[cut:].astype(f32) + back.astype(f32)).astype(bf16)], axis=0)
            else:
                ahead = (to.astype(f32) + ahead.astype(f32)).astype(bf16)
                back = (fro.astype(f32) + back.astype(f32)).astype(bf16)
            ahead, back = self.shift(ahead, 1), self.shift(back, -1)
        return blocks[0].astype(f32) + ahead.astype(f32) + back.astype(f32)


def swap(x):
    return lax.ppermute(x, "col", [(0, 1), (1, 0)])


def turned(x):
    half = x.shape[0] // 2
    return jnp.concatenate([x[half:], x[:half]], axis=0)


FAR = pl.BlockSpec(memory_space=pltpu.HBM)
MARK = jax.ShapeDtypeStruct((8, 128), f32)


def params(mib):
    return pltpu.CompilerParams(vmem_limit_bytes=mib * 2**20)


def cost(*_):
    return pl.CostEstimate(flops=1024, bytes_accessed=1024, transcendentals=0)


def whole(a):
    return pl.BlockSpec(a.shape, lambda i, *_: (0,) * a.ndim)


def mark_spec():
    return pl.BlockSpec(MARK.shape, lambda *_: (0, 0))


def columns(at, width):
    return pl.ds(pl.multiple_of(at * width, 128), width)


def held(x):
    return pltpu.with_memory_space_constraint(x, pltpu.HBM)


def tie(arrays, after):
    count = len(arrays)

    def body(*refs):
        del refs

    return pl.pallas_call(
        body,
        out_shape=[jax.ShapeDtypeStruct(a.shape, a.dtype) for a in arrays],
        in_specs=[FAR] * (count + len(after)),
        out_specs=[FAR] * count,
        input_output_aliases={i: i for i in range(count)},
        compiler_params=params(1),
        cost_estimate=cost(),
    )(*arrays, *after)


def shard_stats(blocks, earlier=None):
    rows, width = blocks[0].shape
    count = len(blocks)
    last = earlier is not None
    known = list(earlier) if last else []
    total = count + len(known)

    def body(*refs):
        stats = []
        for k in range(count):
            block = refs[k][...].astype(f32)
            mean = jnp.sum(block, axis=1, keepdims=True) * (1.0 / width)
            away = block - mean
            spread = jnp.sum(away * away, axis=1, keepdims=True)
            stats.append((mean, spread))
        if not last:
            for k in range(count):
                refs[count + k][...] = jnp.concatenate(stats[k], axis=1)
            return
        stats += [(r[:, :1], r[:, 1:]) for r in refs[count:-1]]
        mean = sum(m for m, _ in stats) * (1.0 / total)
        spread = sum(v for _, v in stats) + width * sum((m - mean) ** 2 for m, _ in stats)
        refs[-1][...] = jnp.concatenate([mean, lax.rsqrt(spread * (1.0 / (total * width)) + norm_eps)], axis=1)

    outputs = 1 if last else count
    return pl.pallas_call(
        body,
        grid=(1,),
        in_specs=[whole(x) for x in list(blocks) + known],
        out_specs=[pl.BlockSpec((rows, 2), lambda i: (0, 0))] * outputs,
        out_shape=[jax.ShapeDtypeStruct((rows, 2), f32)] * outputs,
        compiler_params=params(12),
        cost_estimate=cost(),
    )(*blocks, *known)


def assemble(blocks, came, near, slots, norm=None, after=()):
    n = len(blocks)
    pairs = len(came)
    own, width = came[0].shape
    operands = [held(x) for x in [*blocks, *came]] + (list(norm) if norm else [])

    def body(near_ref, slot_ref, *refs):
        out_ref, mark_ref = refs[-2:]
        mark_ref[...] = jnp.zeros(MARK.shape, f32)
        if norm:
            here, there, gain = refs[n + pairs : n + pairs + 3]
        for j in range(pairs):
            flag = jnp.full((own, width), near_ref[j], jnp.int32) == 1
            kept = jnp.where(flag, refs[j][...].astype(f32), refs[j + pairs][...].astype(f32))
            at = columns(slot_ref[j], width)
            got = refs[n + j][...].astype(f32)
            if norm:
                scale = gain[:, at]
                kept = (kept - here[:, :1]) * here[:, 1:] * scale
                got = (got - there[:, :1]) * there[:, 1:] * scale
            out_ref[:own, at] = kept.astype(bf16)
            out_ref[own:, at] = got.astype(bf16)

    return pl.pallas_call(
        body,
        grid_spec=pltpu.PrefetchScalarGridSpec(
            num_scalar_prefetch=2,
            grid=(1,),
            in_specs=[whole(x) for x in operands] + [FAR] * len(after),
            out_specs=[pl.BlockSpec((2 * own, pairs * width), lambda i, *_: (0, 0)), mark_spec()],
        ),
        out_shape=[jax.ShapeDtypeStruct((2 * own, pairs * width), bf16), MARK],
        compiler_params=params(24),
        cost_estimate=cost(),
    )(near, slots, *operands, *after)


def side_product(left, weight, side, by_rows, turn, after=()):
    rows, depth = left.shape
    width = (weight.shape[0] if by_rows else weight.shape[1]) // 2
    block = 512
    steps = width // block
    half = rows // 2

    def body(side_ref, left_ref, weight_ref, *rest):
        part = contract(left_ref[...], weight_ref[...], 1, 1 if by_rows else 0)
        if turn:
            rest[-2][:half] = part[half:]
            rest[-2][half:] = part[:half]
        else:
            rest[-2][...] = part
        rest[-1][...] = jnp.zeros(MARK.shape, f32)

    if by_rows:
        weight_spec = pl.BlockSpec((block, depth), lambda i, s: (s[0] * steps + i, 0))
    else:
        weight_spec = pl.BlockSpec((depth, block), lambda i, s: (0, s[0] * steps + i))
    return pl.pallas_call(
        body,
        grid_spec=pltpu.PrefetchScalarGridSpec(
            num_scalar_prefetch=1,
            grid=(steps,),
            in_specs=[whole(left), weight_spec] + [FAR] * len(after),
            out_specs=[pl.BlockSpec((rows, block), lambda i, s: (0, i)), mark_spec()],
        ),
        out_shape=[jax.ShapeDtypeStruct((rows, width), f32), MARK],
        compiler_params=params(24),
        cost_estimate=cost(rows, depth, width),
    )(side.reshape(1), left, held(weight), *after)


def gelu_half(kept, came, bias, core, after=()):
    rows, width = kept.shape
    block = 512
    steps = width // block
    half = rows // 2

    def body(core_ref, kept_ref, came_ref, bias_ref, *rest):
        value_ref, turned_ref, slope_ref = rest[-3:]
        value, slope = gelu_parts(kept_ref[...] + came_ref[...] + bias_ref[...])
        value = value.astype(bf16)
        value_ref[...] = value
        turned_ref[:half] = value[half:]
        turned_ref[half:] = value[:half]
        slope_ref[...] = slope

    spec = pl.BlockSpec((rows, block), lambda i, s: (0, i))
    return pl.pallas_call(
        body,
        grid_spec=pltpu.PrefetchScalarGridSpec(
            num_scalar_prefetch=1,
            grid=(steps,),
            in_specs=[spec, spec, pl.BlockSpec((1, block), lambda i, s: (0, s[0] * steps + i))] + [FAR] * len(after),
            out_specs=[spec] * 3,
        ),
        out_shape=[jax.ShapeDtypeStruct((rows, width), t) for t in (bf16, bf16, f32)],
        compiler_params=params(24),
        cost_estimate=cost(),
    )(core.reshape(1), kept, came, bias, *after)


def slope_half(kept, came, slope, after=()):
    rows, width = kept.shape
    block = 512
    half = rows // 2

    def body(kept_ref, came_ref, slope_ref, *rest):
        value_ref, turned_ref, mark_ref = rest[-3:]
        mark_ref[...] = jnp.zeros(MARK.shape, f32)
        value = ((kept_ref[...] + came_ref[...]) * slope_ref[...]).astype(bf16)
        value_ref[...] = value
        turned_ref[:half] = value[half:]
        turned_ref[half:] = value[:half]

    spec = pl.BlockSpec((rows, block), lambda i: (0, i))
    return pl.pallas_call(
        body,
        grid=(width // block,),
        in_specs=[spec] * 3 + [FAR] * len(after),
        out_specs=[spec] * 2 + [mark_spec()],
        out_shape=[jax.ShapeDtypeStruct((rows, width), bf16)] * 2 + [MARK],
        compiler_params=params(24),
        cost_estimate=cost(),
    )(kept, came, slope, *after)


def branch_pairs(own, came, weight, where, first, shard_width, after=()):
    rows, depth = own.shape
    half = rows // 2

    def body(where_ref, own_ref, came_ref, weight_own, weight_came, *rest):
        out = contract(own_ref[...], weight_own[...], 1, 0) + contract(came_ref[...], weight_came[...], 1, 0)
        out = out.astype(bf16)
        rest[-3][0] = out[:half]
        rest[-2][0] = out[half:]
        rest[-1][...] = jnp.zeros(MARK.shape, f32)

    out_spec = pl.BlockSpec((1, half, shard_width), lambda i, s: (i, 0, 0))
    return pl.pallas_call(
        body,
        grid_spec=pltpu.PrefetchScalarGridSpec(
            num_scalar_prefetch=1,
            grid=(2,),
            in_specs=[
                whole(own),
                whole(came),
                pl.BlockSpec((depth, shard_width), lambda i, s: (s[4], s[first + i])),
                pl.BlockSpec((depth, shard_width), lambda i, s: (s[5], s[first + i])),
            ]
            + [FAR] * len(after),
            out_specs=[out_spec] * 2 + [mark_spec()],
        ),
        out_shape=[jax.ShapeDtypeStruct((2, half, shard_width), bf16)] * 2 + [MARK],
        compiler_params=params(24),
        cost_estimate=cost(rows, 2 * depth, 2 * shard_width),
    )(where, own, came, held(weight), held(weight), *after)


def normed_pairs(own, came, weight, gain, normed, where, first, shard_width, small, after=()):
    rows, depth = own.shape
    half = rows // 2
    opening = small is None
    extra = [] if opening else [small]
    n = 8

    def body(where_ref, own_ref, came_ref, weight_own, weight_came, gain_ref, normed_ref, *rest):
        keep_ref, give_ref, small_ref, first_ref, second_ref = rest[-5:]
        step = pl.program_id(0)
        grad = contract(own_ref[...], weight_own[...], 1, 1) + contract(came_ref[...], weight_came[...], 1, 1)
        rounded = grad.astype(bf16)
        keep_ref[0] = rounded[:half]
        give_ref[0] = rounded[half:]
        product = grad * normed_ref[...].astype(f32)

        @pl.when(step == 0)
        def _():
            small_ref[...] = jnp.zeros(small_ref.shape, f32) if opening else rest[0][...]
            first_ref[...] = jnp.zeros(first_ref.shape, f32)
            second_ref[...] = jnp.zeros(second_ref.shape, f32)

        small_ref[pl.ds(where_ref[6 + first + step], 1), :] = jnp.sum(product, axis=0, keepdims=True)
        scaled = grad * gain_ref[...]
        lanes = range(0, shard_width, 128)
        first_ref[...] += sum(scaled[:, k : k + 128] for k in lanes)
        second_ref[...] += sum(product[:, k : k + 128] for k in lanes)

        @pl.when(step == 1)
        def _():
            for at, ref in ((0, first_ref), (256, second_ref)):
                by_token = jnp.sum(ref[...].T, axis=0, keepdims=True)
                small_ref[pl.ds(n + where_ref[4], 1), at : at + half] += by_token[:, :half]
                small_ref[pl.ds(n + where_ref[5], 1), at : at + half] += by_token[:, half:]

    out_spec = pl.BlockSpec((1, half, shard_width), lambda i, s: (i, 0, 0))
    small_spec = pl.BlockSpec((2 * n, shard_width), lambda i, s: (0, 0))
    return pl.pallas_call(
        body,
        grid_spec=pltpu.PrefetchScalarGridSpec(
            num_scalar_prefetch=1,
            grid=(2,),
            in_specs=[
                whole(own),
                whole(came),
                pl.BlockSpec((shard_width, depth), lambda i, s: (s[first + i], s[4])),
                pl.BlockSpec((shard_width, depth), lambda i, s: (s[first + i], s[5])),
                pl.BlockSpec((1, shard_width), lambda i, s: (0, s[first + i])),
                pl.BlockSpec((rows, shard_width), lambda i, s: (0, s[first + i])),
            ]
            + [small_spec] * len(extra)
            + [FAR] * len(after),
            out_specs=[out_spec, out_spec, small_spec],
            scratch_shapes=[pltpu.VMEM((rows, 128), f32)] * 2,
        ),
        out_shape=[
            jax.ShapeDtypeStruct((2, half, shard_width), bf16),
            jax.ShapeDtypeStruct((2, half, shard_width), bf16),
            jax.ShapeDtypeStruct((2 * n, shard_width), f32),
        ],
        compiler_params=params(24),
        cost_estimate=cost(),
    )(where, own, came, held(weight), held(weight), gain, normed, *extra, *after)


def out_grad(left, right, side, part, into, after=()):
    tokens, height = left.shape
    width = right.shape[1]
    block = height // 4
    extra = [] if into is None else [into]

    def body(side_ref, left_ref, right_ref, *rest):
        rest[-2][...] = contract(left_ref[...], right_ref[...], 0, 0).astype(bf16)
        rest[-1][...] = jnp.zeros(MARK.shape, f32)

    return pl.pallas_call(
        body,
        grid_spec=pltpu.PrefetchScalarGridSpec(
            num_scalar_prefetch=1,
            grid=(2,),
            in_specs=[pl.BlockSpec((tokens, block), lambda i, s: (0, 2 * part + i)), whole(right)]
            + [FAR] * (len(extra) + len(after)),
            out_specs=[pl.BlockSpec((block, width), lambda i, s: (4 * s[0] + 2 * part + i, 0)), mark_spec()],
        ),
        out_shape=[pltpu.HBM((2 * height, width), bf16), MARK],
        input_output_aliases={} if into is None else {3: 0},
        compiler_params=params(24),
        cost_estimate=cost(height // 2, tokens, width),
    )(side.reshape(1), left, right, *extra, *after)


def in_grad(left, own, came, core, quarter, into, after=()):
    tokens, height = left.shape
    width = own.shape[1]
    block = height // 8
    extra = [] if into is None else [into]

    def body(core_ref, left_ref, own_ref, came_ref, *rest):
        outs = rest[len(extra) + len(after) :]
        at_own, at_came = columns(core_ref[0], width), columns(1 - core_ref[0], width)
        outs[0][:, at_own] = contract(left_ref[...], own_ref[...], 0, 0).astype(bf16)
        outs[0][:, at_came] = contract(left_ref[...], came_ref[...], 0, 0).astype(bf16)
        outs[1][...] = jnp.zeros(MARK.shape, f32)
        if into is None:

            @pl.when(pl.program_id(0) == 0)
            def _():
                outs[2][:, at_own] = jnp.sum(own_ref[...].astype(f32), axis=0, keepdims=True)
                outs[2][:, at_came] = jnp.sum(came_ref[...].astype(f32), axis=0, keepdims=True)

    out_shape = [pltpu.HBM((height, 2 * width), bf16), MARK]
    out_specs = [pl.BlockSpec((block, 2 * width), lambda i, s: (2 * quarter + i, 0)), mark_spec()]
    if into is None:
        out_shape.append(jax.ShapeDtypeStruct((1, 2 * width), f32))
        out_specs.append(pl.BlockSpec((1, 2 * width), lambda i, s: (0, 0)))
    return pl.pallas_call(
        body,
        grid_spec=pltpu.PrefetchScalarGridSpec(
            num_scalar_prefetch=1,
            grid=(2,),
            in_specs=[pl.BlockSpec((tokens, block), lambda i, s: (0, 2 * quarter + i)), whole(own), whole(came)]
            + [FAR] * (len(extra) + len(after)),
            out_specs=out_specs,
        ),
        out_shape=out_shape,
        input_output_aliases={} if into is None else {4: 0},
        compiler_params=params(24),
        cost_estimate=cost(height // 4, tokens, 2 * width),
    )(core.reshape(1), left, own, came, *extra, *after)


class Sum:
    def __init__(self, ring, near, kept, came, far):
        self.ring, self.near, self.kept, self.came, self.far = ring, near, kept, came, far

    def block(self, near_ref, offset, kept_ref, came_ref):
        sel = near_ref[offset % 4]
        sel = sel if offset < 4 else 1 - sel
        flag = jnp.full(kept_ref.shape[1:], sel, jnp.int32) == 1
        return jnp.where(flag, kept_ref[0].astype(f32), came_ref[0].astype(f32))

    def partial(self, offsets, got, small, after):
        own, width = self.came[0].shape[1:]
        operands, specs = [], []
        for offset, taken in zip(offsets, got):
            pair = offset % 4
            here = [self.kept[pair // 2], self.came[pair // 2]]
            operands += here
            specs += [pl.BlockSpec((1, own, width), lambda i, s, at=pair % 2: (at, 0, 0))] * 2
            if taken is not None:
                operands.append(taken)
                specs.append(whole(taken))
        out_shape = [jax.ShapeDtypeStruct((own, width), bf16) for _ in offsets]
        if small is not None:
            operands += list(small)
            specs += [whole(t) for t in small]
            out_shape.append(jax.ShapeDtypeStruct(small[0].shape, f32))
        out_specs = [whole(o) for o in out_shape] + [mark_spec()]
        out_shape.append(MARK)

        def body(near_ref, *refs):
            refs = list(refs)
            outs = refs[len(operands) + len(after) :]
            for k, (offset, taken) in enumerate(zip(offsets, got)):
                total = self.block(near_ref, offset, refs.pop(0), refs.pop(0))
                if taken is not None:
                    total = total + refs.pop(0)[...].astype(f32)
                outs[k][...] = total.astype(bf16)
            if small is not None:
                outs[-2][...] = refs[0][...] + refs[1][...]
            outs[-1][...] = jnp.zeros(MARK.shape, f32)

        return pl.pallas_call(
            body,
            grid_spec=pltpu.PrefetchScalarGridSpec(
                num_scalar_prefetch=1,
                grid=(1,),
                in_specs=specs + [FAR] * len(after),
                out_specs=out_specs,
            ),
            out_shape=out_shape,
            compiler_params=params(16),
            cost_estimate=cost(),
        )(self.near, *operands, *after)

    def hop(self, k, got, small=None, after=()):
        ways = [self.far] if k == 1 else [0, 1]
        offsets = [(4, 3, 2, 1)[k - 1] if way == 0 else (4, 5, 6, 7)[k - 1] for way in ways]
        outs = self.partial(offsets, [got[way] for way in ways], small, after)
        got = [None, None]
        for way, part in zip(ways, outs):
            got[way] = self.ring.shift(part, 1 if way == 0 else -1)
        return got, outs[len(ways)] if small is not None else None, outs[-1]

    def last(self, near0, got):
        block = jnp.where(near0, self.kept[0][0], self.came[0][0])
        return block.astype(f32) + got[0].astype(f32) + got[1].astype(f32)


def wide(tokens, cotangent, up_weight, up_bias, down_weight, norm_gain):
    tok_count, shard_width = tokens.shape
    n = lax.axis_size("row")
    model_width = n * shard_width
    half_width = model_width // 2
    core = lax.axis_index("col")
    row = lax.axis_index("row")
    ring = Ring(n)
    pairs = n // 2
    first_row = core * pairs

    rows_near = [ring.row_at(j) for j in range(pairs)]
    rows_far = [ring.row_at(j + pairs) for j in range(pairs)]
    near = [(r // pairs) == core for r in rows_near]
    slot = [jnp.where(s, a, b) - first_row for s, a, b in zip(near, rows_near, rows_far)]

    as_float = tokens.astype(f32)
    shard_mean = jnp.mean(as_float, axis=1)
    shard_dev = jnp.sum((as_float - shard_mean[:, None]) ** 2, axis=1)
    own_stats = jnp.stack([shard_mean, shard_dev])
    stats = ring.every(own_stats)
    token_mean = jnp.mean(stats[:, 0], axis=0)
    spread = jnp.sum(stats[:, 1], axis=0) + shard_width * jnp.sum((stats[:, 0] - token_mean) ** 2, axis=0)
    inverse_std = lax.rsqrt(spread / model_width + norm_eps)[:, None]
    whitened = (as_float - token_mean[:, None]) * inverse_std
    gain_local = lax.dynamic_slice_in_dim(norm_gain, row * shard_width, shard_width, 0)
    gain_half = lax.dynamic_slice_in_dim(norm_gain, core * half_width, half_width, 0)
    normed = (whitened * gain_local).astype(bf16)

    def halves(x):
        blocks = ring.gather(x)
        out = jnp.zeros((2 * tok_count, half_width), x.dtype)
        for j in range(pairs):
            keep = jnp.where(near[j], blocks[j], blocks[j + pairs])
            send = jnp.where(near[j], blocks[j + pairs], blocks[j])
            both = jnp.concatenate([keep, swap(send)], axis=0)
            out = lax.dynamic_update_slice(out, both, (0, slot[j] * shard_width))
        return out

    normed_cols = halves(normed)
    cot_cols = halves(cotangent)

    width = up_weight.shape[1]
    mine, theirs = core * (width // 2), (1 - core) * (width // 2)

    def summed(part):
        give = lax.dynamic_slice_in_dim(part, theirs, width // 2, 1)
        own = lax.dynamic_slice_in_dim(part, mine, width // 2, 1)
        return own + swap(turned(give))

    def joined(own):
        other = swap(turned(own))
        return jnp.where(
            core == 0,
            jnp.concatenate([own, other], axis=1),
            jnp.concatenate([other, own], axis=1),
        )

    hidden = summed(jnp.dot(normed_cols, up_weight, preferred_element_type=f32))
    hidden = hidden + lax.dynamic_slice_in_dim(up_bias, mine, width // 2, 0)
    act_grad = summed(contract(cot_cols, down_weight, 1, 1))
    gelu_value, gelu_slope = gelu_parts(hidden)
    activation = joined(gelu_value.astype(bf16))
    hidden_grad = joined((act_grad * gelu_slope).astype(bf16))

    def scattered(part):
        keep, recv = part[:tok_count], swap(part[tok_count:])
        blocks = [None] * n
        for j in range(pairs):
            a = lax.dynamic_slice_in_dim(keep, slot[j] * shard_width, shard_width, 1)
            other_slot = jnp.where(near[j], rows_far[j], rows_near[j]) - (1 - core) * pairs
            b = lax.dynamic_slice_in_dim(recv, other_slot * shard_width, shard_width, 1)
            blocks[j] = jnp.where(near[j], a, b)
            blocks[j + pairs] = jnp.where(near[j], b, a)
        return ring.scatter_sum(blocks)

    branch = scattered(jnp.dot(activation, down_weight, preferred_element_type=f32).astype(bf16))
    block_out = (as_float + branch).astype(bf16)

    normed_half = contract(hidden_grad, up_weight, 1, 1)
    product = normed_half * normed_cols.astype(f32)
    first_part = jnp.sum(normed_half * gain_half, axis=1)
    second_part = jnp.sum(product, axis=1)
    gain_part = jnp.sum(product, axis=0)
    by_token = jnp.stack([first_part, second_part]).reshape(2, 2, tok_count)
    by_token = jnp.where(core == 0, by_token, by_token[:, ::-1])
    gain_full = lax.dynamic_update_slice(jnp.zeros((model_width,), f32), gain_part, (core * half_width,))
    small = jnp.concatenate([by_token.reshape(-1), gain_full])
    small = ring.total(small + swap(small))
    by_token = small[: 4 * tok_count].reshape(2, 2, tok_count)
    by_token = lax.dynamic_index_in_dim(by_token, core, 1, keepdims=False) / model_width
    grad_gain = lax.dynamic_slice_in_dim(small, 4 * tok_count + row * shard_width, shard_width, 0) / gain_local

    normed_grad = scattered(normed_half.astype(bf16))
    grad_out = contract(activation, cot_cols, 0, 0).astype(bf16)
    grad_in = contract(normed_cols, hidden_grad, 0, 0).astype(bf16)
    grad_bias = jnp.sum(hidden_grad.astype(f32), axis=0)
    scaled = normed_grad * gain_local
    grad_x = (
        cotangent.astype(f32)
        + inverse_std * (scaled - by_token[0][:, None] - whitened * by_token[1][:, None])
    ).astype(bf16)
    return (block_out, grad_x, grad_in, grad_out, grad_bias, grad_gain)


def local(tokens, cotangent, up_weight, up_bias, down_weight, norm_gain):
    tok_count, shard_width = tokens.shape
    n = lax.axis_size("row")
    if n != ring_limit:
        return wide(tokens, cotangent, up_weight, up_bias, down_weight, norm_gain)
    model_width = n * shard_width
    half_width = model_width // 2
    core = lax.axis_index("col")
    row = lax.axis_index("row")
    other = 1 - core
    ring = Ring(n)
    pairs = n // 2
    mid = tok_count // 2

    rows_near = [ring.row_at(j) for j in range(pairs)]
    rows_far = [ring.row_at(j + pairs) for j in range(pairs)]
    near = [(r // pairs) == core for r in rows_near]
    rows_here = [jnp.where(s, a, b) for s, a, b in zip(near, rows_near, rows_far)]
    near_flags = jnp.stack([s.astype(jnp.int32) for s in near])
    where = jnp.stack([r - core * pairs for r in rows_here] + [core, other] + rows_here).astype(jnp.int32)
    gain_local = lax.dynamic_slice_in_dim(norm_gain, row * shard_width, shard_width, 0)
    gain_half = lax.dynamic_slice_in_dim(norm_gain, core * half_width, half_width, 0)[None]

    def hop(up, down):
        return ring.shift(up, -1), ring.shift(down, 1)

    def crossed(blocks):
        return [swap(jnp.where(near[j], blocks[j + pairs], blocks[j])) for j in range(pairs)]

    t1 = hop(tokens, tokens)
    s0 = shard_stats([tokens])
    t1 = tie(t1, s0)
    t2 = hop(*t1)
    up_near, down_near = up_weight, down_weight
    s1 = shard_stats(t1)
    t2 = tie(t2, s1)
    t3 = hop(*t2)
    s2 = shard_stats(t2)
    t3 = tie(t3, s2)
    t4 = ring.shift(t3[0], -1)
    late = tie([cotangent], [t3[0]])[0]
    c1 = hop(late, late)
    s3 = shard_stats(t3)
    norms = shard_stats([t4], s0 + s1 + s2 + s3)[0]
    t_blocks = [tokens, t1[0], t2[0], t3[0], t4, t3[1], t2[1], t1[1]]
    normed_cols, mark = assemble(t_blocks, crossed(t_blocks), near_flags, where, (norms, swap(norms), gain_half))

    c1 = tie(c1, [mark])
    c2 = hop(*c1)
    hidden_give, mark = side_product(normed_cols, up_near, other, False, True, after=[c1[0]])
    c2 = tie(c2, [mark])
    c3 = hop(*c2)
    hidden_came = swap(tie([hidden_give], [c2[0]])[0])
    hidden_keep, mark = side_product(normed_cols, up_near, core, False, False, after=[c2[0]])
    c3 = tie(c3, [mark])
    c4 = ring.shift(c3[1], 1)
    act_own, act_turned, slope = gelu_half(hidden_keep, hidden_came, up_bias[None], core, after=[c3[0]])
    act_came = swap(act_turned)
    b1, b1_give, mark = branch_pairs(act_own, act_came, down_near, where, 0, shard_width)
    c4 = tie([c4], [mark])[0]
    c_blocks = [cotangent, c1[0], c2[0], c3[0], c4, c3[1], c2[1], c1[1]]
    cot_cols, _ = assemble(c_blocks, crossed(c_blocks), near_flags, where, after=[mark])

    branch = Sum(ring, near_flags, [b1, None], [swap(b1_give), None], 0)
    got, _, mark = branch.hop(1, [None, None], after=[mark])
    b2, b2_give, mark = branch_pairs(act_own, act_came, down_near, where, 2, shard_width, after=[mark])
    branch.kept[1], branch.came[1] = b2, swap(b2_give)
    grad_give, mark = side_product(cot_cols, down_near, other, True, True, after=[mark])
    got, _, mark = branch.hop(2, got, after=[mark])
    grad_came = swap(tie([grad_give], [mark])[0])
    grad_keep, mark = side_product(cot_cols, down_near, core, True, False, after=[mark])
    got, _, mark = branch.hop(3, got, after=[mark])
    hid_own, hid_turned, mark = slope_half(grad_keep, grad_came, slope, after=[mark])
    hid_came = swap(hid_turned)
    grad_out, mark = out_grad(act_own, cot_cols, core, 0, None, after=[mark])

    n1, n1_give, small = normed_pairs(
        hid_own, hid_came, up_near, gain_half, normed_cols, where, 0, shard_width, None, after=[mark]
    )
    branch_got, _, mark = branch.hop(4, got, after=[small])
    n1_give = tie([n1_give], [mark])[0]
    grad_out, mark = out_grad(act_own, cot_cols, core, 1, grad_out, after=[mark])
    norm = Sum(ring, near_flags, [n1, None], [swap(n1_give), None], 1)
    got, _, mark = norm.hop(1, [None, None], after=[mark])
    n2, n2_give, small = normed_pairs(
        hid_own, hid_came, up_near, gain_half, normed_cols, where, 2, shard_width, small, after=[mark]
    )
    branch_got = tie(branch_got, [small])
    n2_give, small = tie([n2_give, small], [branch_got[0], got[1]])
    norm.kept[1], norm.came[1] = n2, swap(n2_give)
    small_got = swap(small)
    grad_out, mark = out_grad(act_came, cot_cols, other, 0, grad_out, after=[small])
    block_out = (tokens.astype(f32) + branch.last(near[0], branch_got)).astype(bf16)

    def toward(x, step):
        return lax.ppermute(x, "row", [(i, i ^ step) for i in range(n)])

    got, small, mark = norm.hop(2, got, (small, small_got), after=[mark])
    small_got = toward(small, 1)
    grad_out, mark = out_grad(act_came, cot_cols, other, 1, grad_out, after=[mark])
    grad_in, mark, grad_bias = in_grad(normed_cols, hid_own, hid_came, core, 0, None, after=[mark])
    got, small, mark = norm.hop(3, got, (small, small_got), after=[mark])
    small_got = toward(small, 2)
    grad_in, mark = in_grad(normed_cols, hid_own, hid_came, core, 1, grad_in, after=[mark])
    grad_in, mark = in_grad(normed_cols, hid_own, hid_came, core, 2, grad_in, after=[mark])
    got, small, mark = norm.hop(4, got, (small, small_got), after=[mark])
    small_got = toward(small, 4)
    grad_in, mark = in_grad(normed_cols, hid_own, hid_came, core, 3, grad_in, after=[mark])
    got = tie(got, [mark])
    small = small + small_got
    token_mean, inverse_std = norms[:, :1], norms[:, 1:]
    by_token = lax.dynamic_index_in_dim(small, n + core, 0, keepdims=False) / model_width
    by_token = [by_token[:tok_count], by_token[256 : 256 + tok_count]]
    grad_gain = lax.dynamic_index_in_dim(small, row, 0, keepdims=False) / gain_local
    scaled = norm.last(near[0], got) * gain_local
    whitened = (tokens.astype(f32) - token_mean) * inverse_std
    grad_x = (
        cotangent.astype(f32)
        + inverse_std * (scaled - by_token[0][:, None] - whitened * by_token[1][:, None])
    ).astype(bf16)
    return (block_out, grad_x, grad_in, grad_out, grad_bias.reshape(-1), grad_gain)


def solution(mesh):
    return jax.shard_map(
        local,
        mesh=mesh,
        in_specs=(
            P(("groups", "col"), "row"),
            P(("groups", "col"), "row"),
            P("col", "row"),
            P("row"),
            P("row", "col"),
            P(),
        ),
        out_specs=(
            P(("groups", "col"), "row"),
            P(("groups", "col"), "row"),
            P(("groups", "col"), "row"),
            P(("groups", "row"), "col"),
            P(("groups", "row")),
            P(("groups", "row")),
        ),
        check_vma=False,
    )
```

```python
import jax
import jax.numpy as jnp
from jax import lax
from jax.experimental import pallas as pl
from jax.experimental.pallas import tpu as pltpu
from jax.sharding import PartitionSpec as P

norm_eps = 1e-06
root_half = 0.7071067811865476
pdf_scale = 0.3989422804014327
bf16 = jnp.bfloat16
f32 = jnp.float32
ring_limit = 8


def gelu_parts(hidden):
    cumulative = 0.5 * (1.0 + lax.erf(hidden * root_half))
    density = jnp.exp(-0.5 * hidden * hidden) * pdf_scale
    return (hidden * cumulative, cumulative + hidden * density)


def contract(left, right, left_dim, right_dim):
    return lax.dot_general(
        left, right, (((left_dim,), (right_dim,)), ((), ())), preferred_element_type=f32
    )


class Ring:
    def __init__(self, n):
        self.n = n
        self.order = list(range(0, n, 2)) + list(range(n - 1, 0, -2))
        row = lax.axis_index("row")
        half = row // 2
        self.place = jnp.where(row % 2 == 0, half, n - 1 - half)

    def shift(self, x, step):
        n, order = self.n, self.order
        return lax.ppermute(x, "row", [(order[i], order[(i + step) % n]) for i in range(n)])

    def row_at(self, offset):
        n = self.n
        place = (self.place + offset) % n
        return jnp.where(place < n // 2, 2 * place, 2 * (n - 1 - place) + 1)

    def every(self, x):
        n = self.n
        if n > ring_limit:
            return lax.all_gather(x, "row")
        sent = [lax.ppermute(x, "row", [(i, (i + k) % n) for i in range(n)]) for k in range(1, n)]
        return jnp.stack([x] + sent)

    def total(self, x):
        step = 1
        while step < self.n:
            x = x + lax.ppermute(x, "row", [(i, i ^ step) for i in range(self.n)])
            step *= 2
        return x

    def gather(self, x):
        n = self.n
        if n > ring_limit:
            rows = lax.all_gather(x, "row")
            return [lax.dynamic_index_in_dim(rows, self.row_at(k), 0, keepdims=False) for k in range(n)]
        blocks = [None] * n
        blocks[0] = up = down = x
        for k in range(1, n // 2):
            up, down = self.shift(up, -1), self.shift(down, 1)
            blocks[k], blocks[n - k] = up, down
        cut = x.shape[0] // 2
        blocks[n // 2] = jnp.concatenate([self.shift(up[:cut], -1), self.shift(down[cut:], 1)], axis=0)
        return blocks

    def scatter_sum(self, blocks):
        n = self.n
        if n > ring_limit:
            stacked = jnp.stack(blocks)
            offsets = [(self.order.index(r) - self.place) % n for r in range(n)]
            by_row = jnp.stack([lax.dynamic_index_in_dim(stacked, k, 0, keepdims=False) for k in offsets])
            return lax.psum_scatter(by_row.astype(f32), "row", scatter_dimension=0)
        mid = n // 2
        cut = blocks[0].shape[0] // 2
        ahead = self.shift(blocks[mid][:cut], 1)
        back = self.shift(blocks[mid][cut:], -1)
        for k in range(mid - 1, 0, -1):
            to, fro = blocks[k], blocks[n - k]
            if k == mid - 1:
                ahead = jnp.concatenate([(to[:cut].astype(f32) + ahead.astype(f32)).astype(bf16), to[cut:]], axis=0)
                back = jnp.concatenate([fro[:cut], (fro[cut:].astype(f32) + back.astype(f32)).astype(bf16)], axis=0)
            else:
                ahead = (to.astype(f32) + ahead.astype(f32)).astype(bf16)
                back = (fro.astype(f32) + back.astype(f32)).astype(bf16)
            ahead, back = self.shift(ahead, 1), self.shift(back, -1)
        return blocks[0].astype(f32) + ahead.astype(f32) + back.astype(f32)


def swap(x):
    return lax.ppermute(x, "col", [(0, 1), (1, 0)])


def turned(x):
    half = x.shape[0] // 2
    return jnp.concatenate([x[half:], x[:half]], axis=0)


FAR = pl.BlockSpec(memory_space=pltpu.HBM)
MARK = jax.ShapeDtypeStruct((8, 128), f32)


def params(mib):
    return pltpu.CompilerParams(vmem_limit_bytes=mib * 2**20)


def cost(*_):
    return pl.CostEstimate(flops=1024, bytes_accessed=1024, transcendentals=0)


def whole(a):
    return pl.BlockSpec(a.shape, lambda i, *_: (0,) * a.ndim)


def mark_spec():
    return pl.BlockSpec(MARK.shape, lambda *_: (0, 0))


def columns(at, width):
    return pl.ds(pl.multiple_of(at * width, 128), width)


def held(x):
    return pltpu.with_memory_space_constraint(x, pltpu.HBM)


def tie(arrays, after):
    count = len(arrays)

    def body(*refs):
        del refs

    return pl.pallas_call(
        body,
        out_shape=[jax.ShapeDtypeStruct(a.shape, a.dtype) for a in arrays],
        in_specs=[FAR] * (count + len(after)),
        out_specs=[FAR] * count,
        input_output_aliases={i: i for i in range(count)},
        compiler_params=params(1),
        cost_estimate=cost(),
    )(*arrays, *after)


def shard_stats(blocks, earlier=None):
    rows, width = blocks[0].shape
    count = len(blocks)
    last = earlier is not None
    known = list(earlier) if last else []
    total = count + len(known)

    def body(*refs):
        stats = []
        for k in range(count):
            block = refs[k][...].astype(f32)
            mean = jnp.sum(block, axis=1, keepdims=True) * (1.0 / width)
            away = block - mean
            spread = jnp.sum(away * away, axis=1, keepdims=True)
            stats.append((mean, spread))
        if not last:
            for k in range(count):
                refs[count + k][...] = jnp.concatenate(stats[k], axis=1)
            return
        stats += [(r[:, :1], r[:, 1:]) for r in refs[count:-1]]
        mean = sum(m for m, _ in stats) * (1.0 / total)
        spread = sum(v for _, v in stats) + width * sum((m - mean) ** 2 for m, _ in stats)
        refs[-1][...] = jnp.concatenate([mean, lax.rsqrt(spread * (1.0 / (total * width)) + norm_eps)], axis=1)

    outputs = 1 if last else count
    return pl.pallas_call(
        body,
        grid=(1,),
        in_specs=[whole(x) for x in list(blocks) + known],
        out_specs=[pl.BlockSpec((rows, 2), lambda i: (0, 0))] * outputs,
        out_shape=[jax.ShapeDtypeStruct((rows, 2), f32)] * outputs,
        compiler_params=params(12),
        cost_estimate=cost(),
    )(*blocks, *known)


def other_half(blocks, near):
    pairs = len(blocks) // 2
    own, width = blocks[0].shape
    part = own // 2

    def body(near_ref, *refs):
        for j in range(pairs):
            flag = jnp.full((part, width), near_ref[j], jnp.int32) == 1
            chosen = jnp.where(flag, refs[j + pairs][...].astype(f32), refs[j][...].astype(f32))
            refs[-1][j] = chosen.astype(bf16)

    return pl.pallas_call(
        body,
        grid_spec=pltpu.PrefetchScalarGridSpec(
            num_scalar_prefetch=1,
            grid=(2,),
            in_specs=[pl.BlockSpec((part, width), lambda i, s: (i, 0))] * len(blocks),
            out_specs=pl.BlockSpec((pairs, part, width), lambda i, s: (0, i, 0)),
        ),
        out_shape=jax.ShapeDtypeStruct((pairs, own, width), bf16),
        compiler_params=params(16),
        cost_estimate=cost(),
    )(near, *map(held, blocks))


def assemble(blocks, came, near, slots, norm=None, after=()):
    n = len(blocks)
    stacked = not isinstance(came, list)
    pairs = len(blocks) // 2
    own, width = blocks[0].shape
    part = own // 2
    operands = [held(x) for x in [*blocks, *([came] if stacked else came)]] + (list(norm) if norm else [])

    def body(near_ref, slot_ref, *refs):
        out_ref, mark_ref = refs[-2:]
        mark_ref[...] = jnp.zeros(MARK.shape, f32)
        if norm:
            here, there, gain = refs[n + pairs : n + pairs + 3]
        for j in range(pairs):
            flag = jnp.full((part, width), near_ref[j], jnp.int32) == 1
            kept = jnp.where(flag, refs[j][...].astype(f32), refs[j + pairs][...].astype(f32))
            at = columns(slot_ref[j], width)
            got = (refs[n][j] if stacked else refs[n + j][...]).astype(f32)
            if norm:
                scale = gain[:, at]
                kept = (kept - here[:, :1]) * here[:, 1:] * scale
                got = (got - there[:, :1]) * there[:, 1:] * scale
            out_ref[0, :, at] = kept.astype(bf16)
            out_ref[1, :, at] = got.astype(bf16)

    def by_tokens(x):
        return pl.BlockSpec((part, x.shape[1]), lambda i, *_: (i, 0))

    specs = [by_tokens(x) for x in operands]
    if norm:
        specs[-1] = whole(operands[-1])
    if stacked:
        specs[n] = pl.BlockSpec((pairs, part, width), lambda i, *_: (0, i, 0))
    out, mark = pl.pallas_call(
        body,
        grid_spec=pltpu.PrefetchScalarGridSpec(
            num_scalar_prefetch=2,
            grid=(2,),
            in_specs=specs + [FAR] * len(after),
            out_specs=[pl.BlockSpec((2, part, pairs * width), lambda i, *_: (0, i, 0)), mark_spec()],
        ),
        out_shape=[jax.ShapeDtypeStruct((2, own, pairs * width), bf16), MARK],
        compiler_params=params(24),
        cost_estimate=cost(),
    )(near, slots, *operands, *after)
    return out.reshape(2 * own, pairs * width), mark


def side_product(left, weight, side, by_rows, turn, after=()):
    rows, depth = left.shape
    width = (weight.shape[0] if by_rows else weight.shape[1]) // 2
    block = 512
    steps = width // block
    half = rows // 2

    def body(side_ref, left_ref, weight_ref, *rest):
        part = contract(left_ref[...], weight_ref[...], 1, 1 if by_rows else 0)
        if turn:
            rest[-2][:half] = part[half:]
            rest[-2][half:] = part[:half]
        else:
            rest[-2][...] = part
        rest[-1][...] = jnp.zeros(MARK.shape, f32)

    if by_rows:
        weight_spec = pl.BlockSpec((block, depth), lambda i, s: (s[0] * steps + i, 0))
    else:
        weight_spec = pl.BlockSpec((depth, block), lambda i, s: (0, s[0] * steps + i))
    return pl.pallas_call(
        body,
        grid_spec=pltpu.PrefetchScalarGridSpec(
            num_scalar_prefetch=1,
            grid=(steps,),
            in_specs=[whole(left), weight_spec] + [FAR] * len(after),
            out_specs=[pl.BlockSpec((rows, block), lambda i, s: (0, i)), mark_spec()],
        ),
        out_shape=[jax.ShapeDtypeStruct((rows, width), f32), MARK],
        compiler_params=params(24),
        cost_estimate=cost(rows, depth, width),
    )(side.reshape(1), left, held(weight), *after)


def gelu_half(kept, came, bias, core, after=()):
    rows, width = kept.shape
    block = 512
    steps = width // block
    half = rows // 2

    def body(core_ref, kept_ref, came_ref, bias_ref, *rest):
        value_ref, turned_ref, slope_ref = rest[-3:]
        value, slope = gelu_parts(kept_ref[...] + came_ref[...] + bias_ref[...])
        value = value.astype(bf16)
        value_ref[...] = value
        turned_ref[:half] = value[half:]
        turned_ref[half:] = value[:half]
        slope_ref[...] = slope

    spec = pl.BlockSpec((rows, block), lambda i, s: (0, i))
    return pl.pallas_call(
        body,
        grid_spec=pltpu.PrefetchScalarGridSpec(
            num_scalar_prefetch=1,
            grid=(steps,),
            in_specs=[spec, spec, pl.BlockSpec((1, block), lambda i, s: (0, s[0] * steps + i))] + [FAR] * len(after),
            out_specs=[spec] * 3,
        ),
        out_shape=[jax.ShapeDtypeStruct((rows, width), t) for t in (bf16, bf16, f32)],
        compiler_params=params(24),
        cost_estimate=cost(),
    )(core.reshape(1), kept, came, bias, *after)


def slope_half(kept, came, slope, after=()):
    rows, width = kept.shape
    block = 512
    half = rows // 2

    def body(kept_ref, came_ref, slope_ref, *rest):
        value_ref, turned_ref, mark_ref = rest[-3:]
        mark_ref[...] = jnp.zeros(MARK.shape, f32)
        value = ((kept_ref[...] + came_ref[...]) * slope_ref[...]).astype(bf16)
        value_ref[...] = value
        turned_ref[:half] = value[half:]
        turned_ref[half:] = value[:half]

    spec = pl.BlockSpec((rows, block), lambda i: (0, i))
    return pl.pallas_call(
        body,
        grid=(width // block,),
        in_specs=[spec] * 3 + [FAR] * len(after),
        out_specs=[spec] * 2 + [mark_spec()],
        out_shape=[jax.ShapeDtypeStruct((rows, width), bf16)] * 2 + [MARK],
        compiler_params=params(24),
        cost_estimate=cost(),
    )(kept, came, slope, *after)


def branch_pairs(own, came, weight, where, first, shard_width, after=()):
    rows, depth = own.shape
    half = rows // 2

    def body(where_ref, own_ref, came_ref, weight_own, weight_came, *rest):
        out = contract(own_ref[...], weight_own[...], 1, 0) + contract(came_ref[...], weight_came[...], 1, 0)
        out = out.astype(bf16)
        rest[-3][0] = out[:half]
        rest[-2][0] = out[half:]
        rest[-1][...] = jnp.zeros(MARK.shape, f32)

    out_spec = pl.BlockSpec((1, half, shard_width), lambda i, s: (i, 0, 0))
    return pl.pallas_call(
        body,
        grid_spec=pltpu.PrefetchScalarGridSpec(
            num_scalar_prefetch=1,
            grid=(2,),
            in_specs=[
                whole(own),
                whole(came),
                pl.BlockSpec((depth, shard_width), lambda i, s: (s[4], s[first + i])),
                pl.BlockSpec((depth, shard_width), lambda i, s: (s[5], s[first + i])),
            ]
            + [FAR] * len(after),
            out_specs=[out_spec] * 2 + [mark_spec()],
        ),
        out_shape=[jax.ShapeDtypeStruct((2, half, shard_width), bf16)] * 2 + [MARK],
        compiler_params=params(24),
        cost_estimate=cost(rows, 2 * depth, 2 * shard_width),
    )(where, own, came, held(weight), held(weight), *after)


def normed_pairs(own, came, weight, gain, normed, where, first, shard_width, small, after=()):
    rows, depth = own.shape
    half = rows // 2
    opening = small is None
    extra = [] if opening else [small]
    n = 8

    def body(where_ref, own_ref, came_ref, weight_own, weight_came, gain_ref, normed_ref, *rest):
        keep_ref, give_ref, small_ref, first_ref, second_ref = rest[-5:]
        step = pl.program_id(0)
        grad = contract(own_ref[...], weight_own[...], 1, 1) + contract(came_ref[...], weight_came[...], 1, 1)
        rounded = grad.astype(bf16)
        keep_ref[0] = rounded[:half]
        give_ref[0] = rounded[half:]
        product = grad * normed_ref[...].astype(f32)

        @pl.when(step == 0)
        def _():
            small_ref[...] = jnp.zeros(small_ref.shape, f32) if opening else rest[0][...]
            first_ref[...] = jnp.zeros(first_ref.shape, f32)
            second_ref[...] = jnp.zeros(second_ref.shape, f32)

        small_ref[pl.ds(where_ref[6 + first + step], 1), :] = jnp.sum(product, axis=0, keepdims=True)
        scaled = grad * gain_ref[...]
        lanes = range(0, shard_width, 128)
        first_ref[...] += sum(scaled[:, k : k + 128] for k in lanes)
        second_ref[...] += sum(product[:, k : k + 128] for k in lanes)

        @pl.when(step == 1)
        def _():
            for at, ref in ((0, first_ref), (256, second_ref)):
                by_token = jnp.sum(ref[...].T, axis=0, keepdims=True)
                small_ref[pl.ds(n + where_ref[4], 1), at : at + half] += by_token[:, :half]
                small_ref[pl.ds(n + where_ref[5], 1), at : at + half] += by_token[:, half:]

    out_spec = pl.BlockSpec((1, half, shard_width), lambda i, s: (i, 0, 0))
    small_spec = pl.BlockSpec((2 * n, shard_width), lambda i, s: (0, 0))
    return pl.pallas_call(
        body,
        grid_spec=pltpu.PrefetchScalarGridSpec(
            num_scalar_prefetch=1,
            grid=(2,),
            in_specs=[
                whole(own),
                whole(came),
                pl.BlockSpec((shard_width, depth), lambda i, s: (s[first + i], s[4])),
                pl.BlockSpec((shard_width, depth), lambda i, s: (s[first + i], s[5])),
                pl.BlockSpec((1, shard_width), lambda i, s: (0, s[first + i])),
                pl.BlockSpec((rows, shard_width), lambda i, s: (0, s[first + i])),
            ]
            + [small_spec] * len(extra)
            + [FAR] * len(after),
            out_specs=[out_spec, out_spec, small_spec],
            scratch_shapes=[pltpu.VMEM((rows, 128), f32)] * 2,
        ),
        out_shape=[
            jax.ShapeDtypeStruct((2, half, shard_width), bf16),
            jax.ShapeDtypeStruct((2, half, shard_width), bf16),
            jax.ShapeDtypeStruct((2 * n, shard_width), f32),
        ],
        compiler_params=params(24),
        cost_estimate=cost(),
    )(where, own, came, held(weight), held(weight), gain, normed, *extra, *after)


def out_grad(left, right, side, part, into, after=()):
    tokens, height = left.shape
    width = right.shape[1]
    block = height // 4
    extra = [] if into is None else [into]

    def body(side_ref, left_ref, right_ref, *rest):
        rest[-2][...] = contract(left_ref[...], right_ref[...], 0, 0).astype(bf16)
        rest[-1][...] = jnp.zeros(MARK.shape, f32)

    return pl.pallas_call(
        body,
        grid_spec=pltpu.PrefetchScalarGridSpec(
            num_scalar_prefetch=1,
            grid=(2,),
            in_specs=[pl.BlockSpec((tokens, block), lambda i, s: (0, 2 * part + i)), whole(right)]
            + [FAR] * (len(extra) + len(after)),
            out_specs=[pl.BlockSpec((block, width), lambda i, s: (4 * s[0] + 2 * part + i, 0)), mark_spec()],
        ),
        out_shape=[pltpu.HBM((2 * height, width), bf16), MARK],
        input_output_aliases={} if into is None else {3: 0},
        compiler_params=params(24),
        cost_estimate=cost(height // 2, tokens, width),
    )(side.reshape(1), left, right, *extra, *after)


def in_grad(left, own, came, core, part, into, after=()):
    tokens, height = left.shape
    width = own.shape[1]
    block = height // 8
    extra = [] if into is None else [into]

    def body(core_ref, left_ref, own_ref, came_ref, *rest):
        outs = rest[len(extra) + len(after) :]
        at_own, at_came = columns(core_ref[0], width), columns(1 - core_ref[0], width)
        outs[0][:, at_own] = contract(left_ref[...], own_ref[...], 0, 0).astype(bf16)
        outs[0][:, at_came] = contract(left_ref[...], came_ref[...], 0, 0).astype(bf16)
        outs[1][...] = jnp.zeros(MARK.shape, f32)
        if into is None:

            @pl.when(pl.program_id(0) == 0)
            def _():
                outs[2][:, at_own] = jnp.sum(own_ref[...].astype(f32), axis=0, keepdims=True)
                outs[2][:, at_came] = jnp.sum(came_ref[...].astype(f32), axis=0, keepdims=True)

    out_shape = [pltpu.HBM((height, 2 * width), bf16), MARK]
    out_specs = [pl.BlockSpec((block, 2 * width), lambda i, s: (4 * part + i, 0)), mark_spec()]
    if into is None:
        out_shape.append(jax.ShapeDtypeStruct((1, 2 * width), f32))
        out_specs.append(pl.BlockSpec((1, 2 * width), lambda i, s: (0, 0)))
    return pl.pallas_call(
        body,
        grid_spec=pltpu.PrefetchScalarGridSpec(
            num_scalar_prefetch=1,
            grid=(4,),
            in_specs=[pl.BlockSpec((tokens, block), lambda i, s: (0, 4 * part + i)), whole(own), whole(came)]
            + [FAR] * (len(extra) + len(after)),
            out_specs=out_specs,
        ),
        out_shape=out_shape,
        input_output_aliases={} if into is None else {4: 0},
        compiler_params=params(24),
        cost_estimate=cost(height // 4, tokens, 2 * width),
    )(core.reshape(1), left, own, came, *extra, *after)


class Sum:
    def __init__(self, ring, near, kept, came, far):
        self.ring, self.near, self.kept, self.came, self.far = ring, near, kept, came, far

    def block(self, near_ref, offset, kept_ref, came_ref):
        sel = near_ref[offset % 4]
        sel = sel if offset < 4 else 1 - sel
        flag = jnp.full(kept_ref.shape[1:], sel, jnp.int32) == 1
        return jnp.where(flag, kept_ref[0].astype(f32), came_ref[0].astype(f32))

    def partial(self, offsets, got, small, after):
        own, width = self.came[0].shape[1:]
        operands, specs = [], []
        for offset, taken in zip(offsets, got):
            pair = offset % 4
            here = [self.kept[pair // 2], self.came[pair // 2]]
            operands += here
            specs += [pl.BlockSpec((1, own, width), lambda i, s, at=pair % 2: (at, 0, 0))] * 2
            if taken is not None:
                operands.append(taken)
                specs.append(whole(taken))
        out_shape = [jax.ShapeDtypeStruct((own, width), bf16) for _ in offsets]
        if small is not None:
            operands += list(small)
            specs += [whole(t) for t in small]
            out_shape.append(jax.ShapeDtypeStruct(small[0].shape, f32))
        out_specs = [whole(o) for o in out_shape] + [mark_spec()]
        out_shape.append(MARK)

        def body(near_ref, *refs):
            refs = list(refs)
            outs = refs[len(operands) + len(after) :]
            for k, (offset, taken) in enumerate(zip(offsets, got)):
                total = self.block(near_ref, offset, refs.pop(0), refs.pop(0))
                if taken is not None:
                    total = total + refs.pop(0)[...].astype(f32)
                outs[k][...] = total.astype(bf16)
            if small is not None:
                outs[-2][...] = refs[0][...] + refs[1][...]
            outs[-1][...] = jnp.zeros(MARK.shape, f32)

        return pl.pallas_call(
            body,
            grid_spec=pltpu.PrefetchScalarGridSpec(
                num_scalar_prefetch=1,
                grid=(1,),
                in_specs=specs + [FAR] * len(after),
                out_specs=out_specs,
            ),
            out_shape=out_shape,
            compiler_params=params(16),
            cost_estimate=cost(),
        )(self.near, *operands, *after)

    def hop(self, k, got, small=None, after=()):
        ways = [self.far] if k == 1 else [0, 1]
        offsets = [(4, 3, 2, 1)[k - 1] if way == 0 else (4, 5, 6, 7)[k - 1] for way in ways]
        outs = self.partial(offsets, [got[way] for way in ways], small, after)
        got = [None, None]
        for way, part in zip(ways, outs):
            got[way] = self.ring.shift(part, 1 if way == 0 else -1)
        return got, outs[len(ways)] if small is not None else None, outs[-1]

    def last(self, near0, got):
        block = jnp.where(near0, self.kept[0][0], self.came[0][0])
        return block.astype(f32) + got[0].astype(f32) + got[1].astype(f32)


def wide(tokens, cotangent, up_weight, up_bias, down_weight, norm_gain):
    tok_count, shard_width = tokens.shape
    n = lax.axis_size("row")
    model_width = n * shard_width
    half_width = model_width // 2
    core = lax.axis_index("col")
    row = lax.axis_index("row")
    ring = Ring(n)
    pairs = n // 2
    first_row = core * pairs

    rows_near = [ring.row_at(j) for j in range(pairs)]
    rows_far = [ring.row_at(j + pairs) for j in range(pairs)]
    near = [(r // pairs) == core for r in rows_near]
    slot = [jnp.where(s, a, b) - first_row for s, a, b in zip(near, rows_near, rows_far)]

    as_float = tokens.astype(f32)
    shard_mean = jnp.mean(as_float, axis=1)
    shard_dev = jnp.sum((as_float - shard_mean[:, None]) ** 2, axis=1)
    own_stats = jnp.stack([shard_mean, shard_dev])
    stats = ring.every(own_stats)
    token_mean = jnp.mean(stats[:, 0], axis=0)
    spread = jnp.sum(stats[:, 1], axis=0) + shard_width * jnp.sum((stats[:, 0] - token_mean) ** 2, axis=0)
    inverse_std = lax.rsqrt(spread / model_width + norm_eps)[:, None]
    whitened = (as_float - token_mean[:, None]) * inverse_std
    gain_local = lax.dynamic_slice_in_dim(norm_gain, row * shard_width, shard_width, 0)
    gain_half = lax.dynamic_slice_in_dim(norm_gain, core * half_width, half_width, 0)
    normed = (whitened * gain_local).astype(bf16)

    def halves(x):
        blocks = ring.gather(x)
        out = jnp.zeros((2 * tok_count, half_width), x.dtype)
        for j in range(pairs):
            keep = jnp.where(near[j], blocks[j], blocks[j + pairs])
            send = jnp.where(near[j], blocks[j + pairs], blocks[j])
            both = jnp.concatenate([keep, swap(send)], axis=0)
            out = lax.dynamic_update_slice(out, both, (0, slot[j] * shard_width))
        return out

    normed_cols = halves(normed)
    cot_cols = halves(cotangent)

    width = up_weight.shape[1]
    mine, theirs = core * (width // 2), (1 - core) * (width // 2)

    def summed(part):
        give = lax.dynamic_slice_in_dim(part, theirs, width // 2, 1)
        own = lax.dynamic_slice_in_dim(part, mine, width // 2, 1)
        return own + swap(turned(give))

    def joined(own):
        other = swap(turned(own))
        return jnp.where(
            core == 0,
            jnp.concatenate([own, other], axis=1),
            jnp.concatenate([other, own], axis=1),
        )

    hidden = summed(jnp.dot(normed_cols, up_weight, preferred_element_type=f32))
    hidden = hidden + lax.dynamic_slice_in_dim(up_bias, mine, width // 2, 0)
    act_grad = summed(contract(cot_cols, down_weight, 1, 1))
    gelu_value, gelu_slope = gelu_parts(hidden)
    activation = joined(gelu_value.astype(bf16))
    hidden_grad = joined((act_grad * gelu_slope).astype(bf16))

    def scattered(part):
        keep, recv = part[:tok_count], swap(part[tok_count:])
        blocks = [None] * n
        for j in range(pairs):
            a = lax.dynamic_slice_in_dim(keep, slot[j] * shard_width, shard_width, 1)
            other_slot = jnp.where(near[j], rows_far[j], rows_near[j]) - (1 - core) * pairs
            b = lax.dynamic_slice_in_dim(recv, other_slot * shard_width, shard_width, 1)
            blocks[j] = jnp.where(near[j], a, b)
            blocks[j + pairs] = jnp.where(near[j], b, a)
        return ring.scatter_sum(blocks)

    branch = scattered(jnp.dot(activation, down_weight, preferred_element_type=f32).astype(bf16))
    block_out = (as_float + branch).astype(bf16)

    normed_half = contract(hidden_grad, up_weight, 1, 1)
    product = normed_half * normed_cols.astype(f32)
    first_part = jnp.sum(normed_half * gain_half, axis=1)
    second_part = jnp.sum(product, axis=1)
    gain_part = jnp.sum(product, axis=0)
    by_token = jnp.stack([first_part, second_part]).reshape(2, 2, tok_count)
    by_token = jnp.where(core == 0, by_token, by_token[:, ::-1])
    gain_full = lax.dynamic_update_slice(jnp.zeros((model_width,), f32), gain_part, (core * half_width,))
    small = jnp.concatenate([by_token.reshape(-1), gain_full])
    small = ring.total(small + swap(small))
    by_token = small[: 4 * tok_count].reshape(2, 2, tok_count)
    by_token = lax.dynamic_index_in_dim(by_token, core, 1, keepdims=False) / model_width
    grad_gain = lax.dynamic_slice_in_dim(small, 4 * tok_count + row * shard_width, shard_width, 0) / gain_local

    normed_grad = scattered(normed_half.astype(bf16))
    grad_out = contract(activation, cot_cols, 0, 0).astype(bf16)
    grad_in = contract(normed_cols, hidden_grad, 0, 0).astype(bf16)
    grad_bias = jnp.sum(hidden_grad.astype(f32), axis=0)
    scaled = normed_grad * gain_local
    grad_x = (
        cotangent.astype(f32)
        + inverse_std * (scaled - by_token[0][:, None] - whitened * by_token[1][:, None])
    ).astype(bf16)
    return (block_out, grad_x, grad_in, grad_out, grad_bias, grad_gain)


def local(tokens, cotangent, up_weight, up_bias, down_weight, norm_gain):
    tok_count, shard_width = tokens.shape
    n = lax.axis_size("row")
    if n != ring_limit:
        return wide(tokens, cotangent, up_weight, up_bias, down_weight, norm_gain)
    model_width = n * shard_width
    half_width = model_width // 2
    core = lax.axis_index("col")
    row = lax.axis_index("row")
    other = 1 - core
    ring = Ring(n)
    pairs = n // 2
    mid = tok_count // 2

    rows_near = [ring.row_at(j) for j in range(pairs)]
    rows_far = [ring.row_at(j + pairs) for j in range(pairs)]
    near = [(r // pairs) == core for r in rows_near]
    rows_here = [jnp.where(s, a, b) for s, a, b in zip(near, rows_near, rows_far)]
    near_flags = jnp.stack([s.astype(jnp.int32) for s in near])
    where = jnp.stack([r - core * pairs for r in rows_here] + [core, other] + rows_here).astype(jnp.int32)
    gain_local = lax.dynamic_slice_in_dim(norm_gain, row * shard_width, shard_width, 0)
    gain_half = lax.dynamic_slice_in_dim(norm_gain, core * half_width, half_width, 0)[None]

    def hop(up, down):
        return ring.shift(up, -1), ring.shift(down, 1)

    def crossed(blocks):
        return [swap(jnp.where(near[j], blocks[j + pairs], blocks[j])) for j in range(pairs)]

    t1 = hop(tokens, tokens)
    s0 = shard_stats([tokens])
    t1 = tie(t1, s0)
    t2 = hop(*t1)
    up_near, down_near = up_weight, down_weight
    s1 = shard_stats(t1)
    t2 = tie(t2, s1)
    t3 = hop(*t2)
    s2 = shard_stats(t2)
    t3 = tie(t3, s2)
    t4 = ring.shift(t3[0], -1)
    late = tie([cotangent], [t3[0]])[0]
    c1 = hop(late, late)
    s3 = shard_stats(t3)
    norms = shard_stats([t4], s0 + s1 + s2 + s3)[0]
    t_blocks = [tokens, t1[0], t2[0], t3[0], t4, t3[1], t2[1], t1[1]]
    normed_cols, mark = assemble(t_blocks, crossed(t_blocks), near_flags, where, (norms, swap(norms), gain_half))

    c1 = tie(c1, [mark])
    c2 = hop(*c1)
    hidden_give, mark = side_product(normed_cols, up_near, other, False, True, after=[c1[0]])
    c2 = tie(c2, [mark])
    c3 = hop(*c2)
    hidden_came = swap(tie([hidden_give], [c2[0]])[0])
    hidden_keep, mark = side_product(normed_cols, up_near, core, False, False, after=[c2[0]])
    c3 = tie(c3, [mark])
    c4 = ring.shift(c3[1], 1)
    act_own, act_turned, slope = gelu_half(hidden_keep, hidden_came, up_bias[None], core, after=[c3[0]])
    act_came = swap(act_turned)
    b1, b1_give, mark = branch_pairs(act_own, act_came, down_near, where, 0, shard_width)
    c4 = tie([c4], [mark])[0]
    b1_give = tie([b1_give], [c4])[0]
    c_blocks = [cotangent, c1[0], c2[0], c3[0], c4, c3[1], c2[1], c1[1]]
    c_came = swap(other_half(c_blocks, near_flags))

    branch = Sum(ring, near_flags, [b1, None], [swap(b1_give), None], 0)
    got, _, mark = branch.hop(1, [None, None], after=[mark])
    b2, b2_give, mark = branch_pairs(act_own, act_came, down_near, where, 2, shard_width, after=[mark])
    branch.kept[1], branch.came[1] = b2, swap(tie([b2_give], [got[0]])[0])
    cot_cols, mark = assemble(c_blocks, c_came, near_flags, where, after=[mark])
    got, _, mark = branch.hop(2, got, after=[mark])
    grad_give, mark = side_product(cot_cols, down_near, other, True, True, after=[mark])
    got, _, mark = branch.hop(3, got, after=[mark])
    grad_came = swap(tie([grad_give], [mark])[0])
    grad_keep, mark = side_product(cot_cols, down_near, core, True, False, after=[mark])
    branch_got, _, mark = branch.hop(4, got, after=[mark])
    hid_own, hid_turned, mark = slope_half(grad_keep, grad_came, slope, after=[mark])
    hid_came = swap(hid_turned)
    grad_out, mark = out_grad(act_own, cot_cols, core, 0, None, after=[mark])

    n1, n1_give, small = normed_pairs(
        hid_own, hid_came, up_near, gain_half, normed_cols, where, 0, shard_width, None, after=[mark]
    )
    branch_got = tie(branch_got, [small])
    block_out = (tokens.astype(f32) + branch.last(near[0], branch_got)).astype(bf16)
    n1_give = tie([n1_give], branch_got)[0]
    grad_out, mark = out_grad(act_own, cot_cols, core, 1, grad_out, after=[small])
    norm = Sum(ring, near_flags, [n1, None], [swap(n1_give), None], 1)
    got, _, mark = norm.hop(1, [None, None], after=[mark])
    n2, n2_give, small = normed_pairs(
        hid_own, hid_came, up_near, gain_half, normed_cols, where, 2, shard_width, small, after=[mark]
    )
    n2_give, small = tie([n2_give, small], [got[1]])
    norm.kept[1], norm.came[1] = n2, swap(n2_give)
    small_got = swap(small)
    grad_out, mark = out_grad(act_came, cot_cols, other, 0, grad_out, after=[small])

    def toward(x, step):
        return lax.ppermute(x, "row", [(i, i ^ step) for i in range(n)])

    got, small, mark = norm.hop(2, got, (small, small_got), after=[mark])
    small_got = toward(small, 1)
    grad_in, mark, grad_bias = in_grad(normed_cols, hid_own, hid_came, core, 0, None, after=[mark])
    got, small, mark = norm.hop(3, got, (small, small_got), after=[mark])
    small_got = toward(small, 2)
    grad_in, mark = in_grad(normed_cols, hid_own, hid_came, core, 1, grad_in, after=[mark])
    got, small, mark = norm.hop(4, got, (small, small_got), after=[mark])
    small_got = toward(small, 4)
    grad_out, mark = out_grad(act_came, cot_cols, other, 1, grad_out, after=[mark])
    got = tie(got, [mark])
    small = small + small_got
    token_mean, inverse_std = norms[:, :1], norms[:, 1:]
    by_token = lax.dynamic_index_in_dim(small, n + core, 0, keepdims=False) / model_width
    by_token = [by_token[:tok_count], by_token[256 : 256 + tok_count]]
    grad_gain = lax.dynamic_index_in_dim(small, row, 0, keepdims=False) / gain_local
    scaled = norm.last(near[0], got) * gain_local
    whitened = (tokens.astype(f32) - token_mean) * inverse_std
    grad_x = (
        cotangent.astype(f32)
        + inverse_std * (scaled - by_token[0][:, None] - whitened * by_token[1][:, None])
    ).astype(bf16)
    return (block_out, grad_x, grad_in, grad_out, grad_bias.reshape(-1), grad_gain)


def solution(mesh):
    return jax.shard_map(
        local,
        mesh=mesh,
        in_specs=(
            P(("groups", "col"), "row"),
            P(("groups", "col"), "row"),
            P("col", "row"),
            P("row"),
            P("row", "col"),
            P(),
        ),
        out_specs=(
            P(("groups", "col"), "row"),
            P(("groups", "col"), "row"),
            P(("groups", "col"), "row"),
            P(("groups", "row"), "col"),
            P(("groups", "row")),
            P(("groups", "row")),
        ),
        check_vma=False,
    )
```

```python
import jax
import jax.numpy as jnp
from jax import lax
from jax.experimental import pallas as pl
from jax.experimental.pallas import tpu as pltpu
from jax.sharding import PartitionSpec as P

norm_eps = 1e-06
root_half = 0.7071067811865476
pdf_scale = 0.3989422804014327
bf16 = jnp.bfloat16
f32 = jnp.float32
ring_limit = 8


def gelu_parts(hidden):
    cumulative = 0.5 * (1.0 + lax.erf(hidden * root_half))
    density = jnp.exp(-0.5 * hidden * hidden) * pdf_scale
    return (hidden * cumulative, cumulative + hidden * density)


def contract(left, right, left_dim, right_dim):
    return lax.dot_general(
        left, right, (((left_dim,), (right_dim,)), ((), ())), preferred_element_type=f32
    )


class Ring:
    def __init__(self, n):
        self.n = n
        self.order = list(range(0, n, 2)) + list(range(n - 1, 0, -2))
        row = lax.axis_index("row")
        half = row // 2
        self.place = jnp.where(row % 2 == 0, half, n - 1 - half)

    def shift(self, x, step):
        n, order = self.n, self.order
        return lax.ppermute(x, "row", [(order[i], order[(i + step) % n]) for i in range(n)])

    def row_at(self, offset):
        n = self.n
        place = (self.place + offset) % n
        return jnp.where(place < n // 2, 2 * place, 2 * (n - 1 - place) + 1)

    def every(self, x):
        n = self.n
        if n > ring_limit:
            return lax.all_gather(x, "row")
        sent = [lax.ppermute(x, "row", [(i, (i + k) % n) for i in range(n)]) for k in range(1, n)]
        return jnp.stack([x] + sent)

    def total(self, x):
        step = 1
        while step < self.n:
            x = x + lax.ppermute(x, "row", [(i, i ^ step) for i in range(self.n)])
            step *= 2
        return x

    def gather(self, x):
        n = self.n
        if n > ring_limit:
            rows = lax.all_gather(x, "row")
            return [lax.dynamic_index_in_dim(rows, self.row_at(k), 0, keepdims=False) for k in range(n)]
        blocks = [None] * n
        blocks[0] = up = down = x
        for k in range(1, n // 2):
            up, down = self.shift(up, -1), self.shift(down, 1)
            blocks[k], blocks[n - k] = up, down
        cut = x.shape[0] // 2
        blocks[n // 2] = jnp.concatenate([self.shift(up[:cut], -1), self.shift(down[cut:], 1)], axis=0)
        return blocks

    def scatter_sum(self, blocks):
        n = self.n
        if n > ring_limit:
            stacked = jnp.stack(blocks)
            offsets = [(self.order.index(r) - self.place) % n for r in range(n)]
            by_row = jnp.stack([lax.dynamic_index_in_dim(stacked, k, 0, keepdims=False) for k in offsets])
            return lax.psum_scatter(by_row.astype(f32), "row", scatter_dimension=0)
        mid = n // 2
        cut = blocks[0].shape[0] // 2
        ahead = self.shift(blocks[mid][:cut], 1)
        back = self.shift(blocks[mid][cut:], -1)
        for k in range(mid - 1, 0, -1):
            to, fro = blocks[k], blocks[n - k]
            if k == mid - 1:
                ahead = jnp.concatenate([(to[:cut].astype(f32) + ahead.astype(f32)).astype(bf16), to[cut:]], axis=0)
                back = jnp.concatenate([fro[:cut], (fro[cut:].astype(f32) + back.astype(f32)).astype(bf16)], axis=0)
            else:
                ahead = (to.astype(f32) + ahead.astype(f32)).astype(bf16)
                back = (fro.astype(f32) + back.astype(f32)).astype(bf16)
            ahead, back = self.shift(ahead, 1), self.shift(back, -1)
        return blocks[0].astype(f32) + ahead.astype(f32) + back.astype(f32)


def swap(x):
    return lax.ppermute(x, "col", [(0, 1), (1, 0)])


def turned(x):
    half = x.shape[0] // 2
    return jnp.concatenate([x[half:], x[:half]], axis=0)


FAR = pl.BlockSpec(memory_space=pltpu.HBM)
MARK = jax.ShapeDtypeStruct((8, 128), f32)


def params(mib):
    return pltpu.CompilerParams(vmem_limit_bytes=mib * 2**20)


def cost(*_):
    return pl.CostEstimate(flops=1024, bytes_accessed=1024, transcendentals=0)


def whole(a):
    return pl.BlockSpec(a.shape, lambda i, *_: (0,) * a.ndim)


def mark_spec():
    return pl.BlockSpec(MARK.shape, lambda *_: (0, 0))


def columns(at, width):
    return pl.ds(pl.multiple_of(at * width, 128), width)


def held(x):
    return pltpu.with_memory_space_constraint(x, pltpu.HBM)


def tie(arrays, after):
    count = len(arrays)

    def body(*refs):
        del refs

    return pl.pallas_call(
        body,
        out_shape=[jax.ShapeDtypeStruct(a.shape, a.dtype) for a in arrays],
        in_specs=[FAR] * (count + len(after)),
        out_specs=[FAR] * count,
        input_output_aliases={i: i for i in range(count)},
        compiler_params=params(1),
        cost_estimate=cost(),
    )(*arrays, *after)


def shard_stats(blocks, earlier=None):
    rows, width = blocks[0].shape
    count = len(blocks)
    last = earlier is not None
    known = list(earlier) if last else []
    total = count + len(known)

    def body(*refs):
        stats = []
        for k in range(count):
            block = refs[k][...].astype(f32)
            mean = jnp.sum(block, axis=1, keepdims=True) * (1.0 / width)
            away = block - mean
            spread = jnp.sum(away * away, axis=1, keepdims=True)
            stats.append((mean, spread))
        if not last:
            for k in range(count):
                refs[count + k][...] = jnp.concatenate(stats[k], axis=1)
            return
        stats += [(r[:, :1], r[:, 1:]) for r in refs[count:-1]]
        mean = sum(m for m, _ in stats) * (1.0 / total)
        spread = sum(v for _, v in stats) + width * sum((m - mean) ** 2 for m, _ in stats)
        refs[-1][...] = jnp.concatenate([mean, lax.rsqrt(spread * (1.0 / (total * width)) + norm_eps)], axis=1)

    outputs = 1 if last else count
    return pl.pallas_call(
        body,
        grid=(1,),
        in_specs=[whole(x) for x in list(blocks) + known],
        out_specs=[pl.BlockSpec((rows, 2), lambda i: (0, 0))] * outputs,
        out_shape=[jax.ShapeDtypeStruct((rows, 2), f32)] * outputs,
        compiler_params=params(12),
        cost_estimate=cost(),
    )(*blocks, *known)


def other_half(blocks, near):
    pairs = len(blocks) // 2
    own, width = blocks[0].shape
    part = own // 2

    def body(near_ref, *refs):
        for j in range(pairs):
            flag = jnp.full((part, width), near_ref[j], jnp.int32) == 1
            chosen = jnp.where(flag, refs[j + pairs][...].astype(f32), refs[j][...].astype(f32))
            refs[-1][j] = chosen.astype(bf16)

    return pl.pallas_call(
        body,
        grid_spec=pltpu.PrefetchScalarGridSpec(
            num_scalar_prefetch=1,
            grid=(2,),
            in_specs=[pl.BlockSpec((part, width), lambda i, s: (i, 0))] * len(blocks),
            out_specs=pl.BlockSpec((pairs, part, width), lambda i, s: (0, i, 0)),
        ),
        out_shape=jax.ShapeDtypeStruct((pairs, own, width), bf16),
        compiler_params=params(16),
        cost_estimate=cost(),
    )(near, *map(held, blocks))


def assemble(blocks, came, near, slots, norm=None, after=()):
    n = len(blocks)
    stacked = not isinstance(came, list)
    pairs = len(blocks) // 2
    own, width = blocks[0].shape
    part = own // 2
    operands = [held(x) for x in [*blocks, *([came] if stacked else came)]] + (list(norm) if norm else [])

    def body(near_ref, slot_ref, *refs):
        out_ref, mark_ref = refs[-2:]
        mark_ref[...] = jnp.zeros(MARK.shape, f32)
        if norm:
            here, there, gain = refs[n + pairs : n + pairs + 3]
        for j in range(pairs):
            flag = jnp.full((part, width), near_ref[j], jnp.int32) == 1
            kept = jnp.where(flag, refs[j][...].astype(f32), refs[j + pairs][...].astype(f32))
            at = columns(slot_ref[j], width)
            got = (refs[n][j] if stacked else refs[n + j][...]).astype(f32)
            if norm:
                scale = gain[:, at]
                kept = (kept - here[:, :1]) * here[:, 1:] * scale
                got = (got - there[:, :1]) * there[:, 1:] * scale
            out_ref[0, :, at] = kept.astype(bf16)
            out_ref[1, :, at] = got.astype(bf16)

    def by_tokens(x):
        return pl.BlockSpec((part, x.shape[1]), lambda i, *_: (i, 0))

    specs = [by_tokens(x) for x in operands]
    if norm:
        specs[-1] = whole(operands[-1])
    if stacked:
        specs[n] = pl.BlockSpec((pairs, part, width), lambda i, *_: (0, i, 0))
    out, mark = pl.pallas_call(
        body,
        grid_spec=pltpu.PrefetchScalarGridSpec(
            num_scalar_prefetch=2,
            grid=(2,),
            in_specs=specs + [FAR] * len(after),
            out_specs=[pl.BlockSpec((2, part, pairs * width), lambda i, *_: (0, i, 0)), mark_spec()],
        ),
        out_shape=[jax.ShapeDtypeStruct((2, own, pairs * width), bf16), MARK],
        compiler_params=params(24),
        cost_estimate=cost(),
    )(near, slots, *operands, *after)
    return out.reshape(2 * own, pairs * width), mark


def side_product(left, weight, side, by_rows, turn, after=()):
    rows, depth = left.shape
    width = (weight.shape[0] if by_rows else weight.shape[1]) // 2
    block = 512
    steps = width // block
    half = rows // 2

    def body(side_ref, left_ref, weight_ref, *rest):
        part = contract(left_ref[...], weight_ref[...], 1, 1 if by_rows else 0)
        if turn:
            rest[-2][:half] = part[half:]
            rest[-2][half:] = part[:half]
        else:
            rest[-2][...] = part
        rest[-1][...] = jnp.zeros(MARK.shape, f32)

    if by_rows:
        weight_spec = pl.BlockSpec((block, depth), lambda i, s: (s[0] * steps + i, 0))
    else:
        weight_spec = pl.BlockSpec((depth, block), lambda i, s: (0, s[0] * steps + i))
    return pl.pallas_call(
        body,
        grid_spec=pltpu.PrefetchScalarGridSpec(
            num_scalar_prefetch=1,
            grid=(steps,),
            in_specs=[whole(left), weight_spec] + [FAR] * len(after),
            out_specs=[pl.BlockSpec((rows, block), lambda i, s: (0, i)), mark_spec()],
        ),
        out_shape=[jax.ShapeDtypeStruct((rows, width), f32), MARK],
        compiler_params=params(24),
        cost_estimate=cost(rows, depth, width),
    )(side.reshape(1), left, held(weight), *after)


def gelu_half(kept, came, bias, core, after=()):
    rows, width = kept.shape
    block = 512
    steps = width // block
    half = rows // 2

    def body(core_ref, kept_ref, came_ref, bias_ref, *rest):
        value_ref, turned_ref, slope_ref = rest[-3:]
        value, slope = gelu_parts(kept_ref[...] + came_ref[...] + bias_ref[...])
        value = value.astype(bf16)
        value_ref[...] = value
        turned_ref[:half] = value[half:]
        turned_ref[half:] = value[:half]
        slope_ref[...] = slope

    spec = pl.BlockSpec((rows, block), lambda i, s: (0, i))
    return pl.pallas_call(
        body,
        grid_spec=pltpu.PrefetchScalarGridSpec(
            num_scalar_prefetch=1,
            grid=(steps,),
            in_specs=[spec, spec, pl.BlockSpec((1, block), lambda i, s: (0, s[0] * steps + i))] + [FAR] * len(after),
            out_specs=[spec] * 3,
        ),
        out_shape=[jax.ShapeDtypeStruct((rows, width), t) for t in (bf16, bf16, f32)],
        compiler_params=params(24),
        cost_estimate=cost(),
    )(core.reshape(1), kept, came, bias, *after)


def slope_half(kept, came, slope, after=()):
    rows, width = kept.shape
    block = 512
    half = rows // 2

    def body(kept_ref, came_ref, slope_ref, *rest):
        value_ref, turned_ref, mark_ref = rest[-3:]
        mark_ref[...] = jnp.zeros(MARK.shape, f32)
        value = ((kept_ref[...] + came_ref[...]) * slope_ref[...]).astype(bf16)
        value_ref[...] = value
        turned_ref[:half] = value[half:]
        turned_ref[half:] = value[:half]

    spec = pl.BlockSpec((rows, block), lambda i: (0, i))
    return pl.pallas_call(
        body,
        grid=(width // block,),
        in_specs=[spec] * 3 + [FAR] * len(after),
        out_specs=[spec] * 2 + [mark_spec()],
        out_shape=[jax.ShapeDtypeStruct((rows, width), bf16)] * 2 + [MARK],
        compiler_params=params(24),
        cost_estimate=cost(),
    )(kept, came, slope, *after)


def branch_pairs(own, came, weight, where, first, shard_width, after=()):
    rows, depth = own.shape
    half = rows // 2

    def body(where_ref, own_ref, came_ref, weight_own, weight_came, *rest):
        out = contract(own_ref[...], weight_own[...], 1, 0) + contract(came_ref[...], weight_came[...], 1, 0)
        out = out.astype(bf16)
        rest[-3][0] = out[:half]
        rest[-2][0] = out[half:]
        rest[-1][...] = jnp.zeros(MARK.shape, f32)

    out_spec = pl.BlockSpec((1, half, shard_width), lambda i, s: (i, 0, 0))
    return pl.pallas_call(
        body,
        grid_spec=pltpu.PrefetchScalarGridSpec(
            num_scalar_prefetch=1,
            grid=(2,),
            in_specs=[
                whole(own),
                whole(came),
                pl.BlockSpec((depth, shard_width), lambda i, s: (s[4], s[first + i])),
                pl.BlockSpec((depth, shard_width), lambda i, s: (s[5], s[first + i])),
            ]
            + [FAR] * len(after),
            out_specs=[out_spec] * 2 + [mark_spec()],
        ),
        out_shape=[jax.ShapeDtypeStruct((2, half, shard_width), bf16)] * 2 + [MARK],
        compiler_params=params(24),
        cost_estimate=cost(rows, 2 * depth, 2 * shard_width),
    )(where, own, came, held(weight), held(weight), *after)


def normed_pairs(own, came, weight, gain, normed, where, first, shard_width, small, after=()):
    rows, depth = own.shape
    half = rows // 2
    opening = small is None
    extra = [] if opening else [small]
    n = 8

    def body(where_ref, own_ref, came_ref, weight_own, weight_came, gain_ref, normed_ref, *rest):
        keep_ref, give_ref, small_ref, first_ref, second_ref = rest[-5:]
        step = pl.program_id(0)
        grad = contract(own_ref[...], weight_own[...], 1, 1) + contract(came_ref[...], weight_came[...], 1, 1)
        rounded = grad.astype(bf16)
        keep_ref[0] = rounded[:half]
        give_ref[0] = rounded[half:]
        product = grad * normed_ref[...].astype(f32)

        @pl.when(step == 0)
        def _():
            small_ref[...] = jnp.zeros(small_ref.shape, f32) if opening else rest[0][...]
            first_ref[...] = jnp.zeros(first_ref.shape, f32)
            second_ref[...] = jnp.zeros(second_ref.shape, f32)

        small_ref[pl.ds(where_ref[6 + first + step], 1), :] = jnp.sum(product, axis=0, keepdims=True)
        scaled = grad * gain_ref[...]
        lanes = range(0, shard_width, 128)
        first_ref[...] += sum(scaled[:, k : k + 128] for k in lanes)
        second_ref[...] += sum(product[:, k : k + 128] for k in lanes)

        @pl.when(step == 1)
        def _():
            for at, ref in ((0, first_ref), (256, second_ref)):
                by_token = jnp.sum(ref[...].T, axis=0, keepdims=True)
                small_ref[pl.ds(n + where_ref[4], 1), at : at + half] += by_token[:, :half]
                small_ref[pl.ds(n + where_ref[5], 1), at : at + half] += by_token[:, half:]

    out_spec = pl.BlockSpec((1, half, shard_width), lambda i, s: (i, 0, 0))
    small_spec = pl.BlockSpec((2 * n, shard_width), lambda i, s: (0, 0))
    return pl.pallas_call(
        body,
        grid_spec=pltpu.PrefetchScalarGridSpec(
            num_scalar_prefetch=1,
            grid=(2,),
            in_specs=[
                whole(own),
                whole(came),
                pl.BlockSpec((shard_width, depth), lambda i, s: (s[first + i], s[4])),
                pl.BlockSpec((shard_width, depth), lambda i, s: (s[first + i], s[5])),
                pl.BlockSpec((1, shard_width), lambda i, s: (0, s[first + i])),
                pl.BlockSpec((rows, shard_width), lambda i, s: (0, s[first + i])),
            ]
            + [small_spec] * len(extra)
            + [FAR] * len(after),
            out_specs=[out_spec, out_spec, small_spec],
            scratch_shapes=[pltpu.VMEM((rows, 128), f32)] * 2,
        ),
        out_shape=[
            jax.ShapeDtypeStruct((2, half, shard_width), bf16),
            jax.ShapeDtypeStruct((2, half, shard_width), bf16),
            jax.ShapeDtypeStruct((2 * n, shard_width), f32),
        ],
        compiler_params=params(24),
        cost_estimate=cost(),
    )(where, own, came, held(weight), held(weight), gain, normed, *extra, *after)


def out_grad(left, right, side, part, into, after=()):
    tokens, height = left.shape
    width = right.shape[1]
    block = height // 4
    extra = [] if into is None else [into]

    def body(side_ref, left_ref, right_ref, *rest):
        rest[-2][...] = contract(left_ref[...], right_ref[...], 0, 0).astype(bf16)
        rest[-1][...] = jnp.zeros(MARK.shape, f32)

    return pl.pallas_call(
        body,
        grid_spec=pltpu.PrefetchScalarGridSpec(
            num_scalar_prefetch=1,
            grid=(2,),
            in_specs=[pl.BlockSpec((tokens, block), lambda i, s: (0, 2 * part + i)), whole(right)]
            + [FAR] * (len(extra) + len(after)),
            out_specs=[pl.BlockSpec((block, width), lambda i, s: (4 * s[0] + 2 * part + i, 0)), mark_spec()],
        ),
        out_shape=[pltpu.HBM((2 * height, width), bf16), MARK],
        input_output_aliases={} if into is None else {3: 0},
        compiler_params=params(24),
        cost_estimate=cost(height // 2, tokens, width),
    )(side.reshape(1), left, right, *extra, *after)


def in_grad(left, own, came, core, part, into, after=()):
    tokens, height = left.shape
    width = own.shape[1]
    block = height // 8
    extra = [] if into is None else [into]

    def body(core_ref, left_ref, own_ref, came_ref, *rest):
        outs = rest[len(extra) + len(after) :]
        at_own, at_came = columns(core_ref[0], width), columns(1 - core_ref[0], width)
        outs[0][:, at_own] = contract(left_ref[...], own_ref[...], 0, 0).astype(bf16)
        outs[0][:, at_came] = contract(left_ref[...], came_ref[...], 0, 0).astype(bf16)
        outs[1][...] = jnp.zeros(MARK.shape, f32)
        if into is None:

            @pl.when(pl.program_id(0) == 0)
            def _():
                outs[2][:, at_own] = jnp.sum(own_ref[...].astype(f32), axis=0, keepdims=True)
                outs[2][:, at_came] = jnp.sum(came_ref[...].astype(f32), axis=0, keepdims=True)

    out_shape = [pltpu.HBM((height, 2 * width), bf16), MARK]
    out_specs = [pl.BlockSpec((block, 2 * width), lambda i, s: (4 * part + i, 0)), mark_spec()]
    if into is None:
        out_shape.append(jax.ShapeDtypeStruct((1, 2 * width), f32))
        out_specs.append(pl.BlockSpec((1, 2 * width), lambda i, s: (0, 0)))
    return pl.pallas_call(
        body,
        grid_spec=pltpu.PrefetchScalarGridSpec(
            num_scalar_prefetch=1,
            grid=(4,),
            in_specs=[pl.BlockSpec((tokens, block), lambda i, s: (0, 4 * part + i)), whole(own), whole(came)]
            + [FAR] * (len(extra) + len(after)),
            out_specs=out_specs,
        ),
        out_shape=out_shape,
        input_output_aliases={} if into is None else {4: 0},
        compiler_params=params(24),
        cost_estimate=cost(height // 4, tokens, 2 * width),
    )(core.reshape(1), left, own, came, *extra, *after)


class Sum:
    def __init__(self, ring, near, kept, came, far):
        self.ring, self.near, self.kept, self.came, self.far = ring, near, kept, came, far

    def block(self, near_ref, offset, kept_ref, came_ref):
        sel = near_ref[offset % 4]
        sel = sel if offset < 4 else 1 - sel
        flag = jnp.full(kept_ref.shape[1:], sel, jnp.int32) == 1
        return jnp.where(flag, kept_ref[0].astype(f32), came_ref[0].astype(f32))

    def partial(self, offsets, got, small, after):
        own, width = self.came[0].shape[1:]
        operands, specs = [], []
        for offset, taken in zip(offsets, got):
            pair = offset % 4
            here = [self.kept[pair // 2], self.came[pair // 2]]
            operands += here
            specs += [pl.BlockSpec((1, own, width), lambda i, s, at=pair % 2: (at, 0, 0))] * 2
            if taken is not None:
                operands.append(taken)
                specs.append(whole(taken))
        out_shape = [jax.ShapeDtypeStruct((own, width), bf16) for _ in offsets]
        if small is not None:
            operands += list(small)
            specs += [whole(t) for t in small]
            out_shape.append(jax.ShapeDtypeStruct(small[0].shape, f32))
        out_specs = [whole(o) for o in out_shape] + [mark_spec()]
        out_shape.append(MARK)

        def body(near_ref, *refs):
            refs = list(refs)
            outs = refs[len(operands) + len(after) :]
            for k, (offset, taken) in enumerate(zip(offsets, got)):
                total = self.block(near_ref, offset, refs.pop(0), refs.pop(0))
                if taken is not None:
                    total = total + refs.pop(0)[...].astype(f32)
                outs[k][...] = total.astype(bf16)
            if small is not None:
                outs[-2][...] = refs[0][...] + refs[1][...]
            outs[-1][...] = jnp.zeros(MARK.shape, f32)

        return pl.pallas_call(
            body,
            grid_spec=pltpu.PrefetchScalarGridSpec(
                num_scalar_prefetch=1,
                grid=(1,),
                in_specs=specs + [FAR] * len(after),
                out_specs=out_specs,
            ),
            out_shape=out_shape,
            compiler_params=params(16),
            cost_estimate=cost(),
        )(self.near, *operands, *after)

    def hop(self, k, got, small=None, after=()):
        ways = [self.far] if k == 1 else [0, 1]
        offsets = [(4, 3, 2, 1)[k - 1] if way == 0 else (4, 5, 6, 7)[k - 1] for way in ways]
        outs = self.partial(offsets, [got[way] for way in ways], small, after)
        got = [None, None]
        for way, part in zip(ways, outs):
            got[way] = self.ring.shift(part, 1 if way == 0 else -1)
        return got, outs[len(ways)] if small is not None else None, outs[-1]

    def last(self, near0, got):
        block = jnp.where(near0, self.kept[0][0], self.came[0][0])
        return block.astype(f32) + got[0].astype(f32) + got[1].astype(f32)


def wide(tokens, cotangent, up_weight, up_bias, down_weight, norm_gain):
    tok_count, shard_width = tokens.shape
    n = lax.axis_size("row")
    model_width = n * shard_width
    half_width = model_width // 2
    core = lax.axis_index("col")
    row = lax.axis_index("row")
    ring = Ring(n)
    pairs = n // 2
    first_row = core * pairs

    rows_near = [ring.row_at(j) for j in range(pairs)]
    rows_far = [ring.row_at(j + pairs) for j in range(pairs)]
    near = [(r // pairs) == core for r in rows_near]
    slot = [jnp.where(s, a, b) - first_row for s, a, b in zip(near, rows_near, rows_far)]

    as_float = tokens.astype(f32)
    shard_mean = jnp.mean(as_float, axis=1)
    shard_dev = jnp.sum((as_float - shard_mean[:, None]) ** 2, axis=1)
    own_stats = jnp.stack([shard_mean, shard_dev])
    stats = ring.every(own_stats)
    token_mean = jnp.mean(stats[:, 0], axis=0)
    spread = jnp.sum(stats[:, 1], axis=0) + shard_width * jnp.sum((stats[:, 0] - token_mean) ** 2, axis=0)
    inverse_std = lax.rsqrt(spread / model_width + norm_eps)[:, None]
    whitened = (as_float - token_mean[:, None]) * inverse_std
    gain_local = lax.dynamic_slice_in_dim(norm_gain, row * shard_width, shard_width, 0)
    gain_half = lax.dynamic_slice_in_dim(norm_gain, core * half_width, half_width, 0)
    normed = (whitened * gain_local).astype(bf16)

    def halves(x):
        blocks = ring.gather(x)
        out = jnp.zeros((2 * tok_count, half_width), x.dtype)
        for j in range(pairs):
            keep = jnp.where(near[j], blocks[j], blocks[j + pairs])
            send = jnp.where(near[j], blocks[j + pairs], blocks[j])
            both = jnp.concatenate([keep, swap(send)], axis=0)
            out = lax.dynamic_update_slice(out, both, (0, slot[j] * shard_width))
        return out

    normed_cols = halves(normed)
    cot_cols = halves(cotangent)

    width = up_weight.shape[1]
    mine, theirs = core * (width // 2), (1 - core) * (width // 2)

    def summed(part):
        give = lax.dynamic_slice_in_dim(part, theirs, width // 2, 1)
        own = lax.dynamic_slice_in_dim(part, mine, width // 2, 1)
        return own + swap(turned(give))

    def joined(own):
        other = swap(turned(own))
        return jnp.where(
            core == 0,
            jnp.concatenate([own, other], axis=1),
            jnp.concatenate([other, own], axis=1),
        )

    hidden = summed(jnp.dot(normed_cols, up_weight, preferred_element_type=f32))
    hidden = hidden + lax.dynamic_slice_in_dim(up_bias, mine, width // 2, 0)
    act_grad = summed(contract(cot_cols, down_weight, 1, 1))
    gelu_value, gelu_slope = gelu_parts(hidden)
    activation = joined(gelu_value.astype(bf16))
    hidden_grad = joined((act_grad * gelu_slope).astype(bf16))

    def scattered(part):
        keep, recv = part[:tok_count], swap(part[tok_count:])
        blocks = [None] * n
        for j in range(pairs):
            a = lax.dynamic_slice_in_dim(keep, slot[j] * shard_width, shard_width, 1)
            other_slot = jnp.where(near[j], rows_far[j], rows_near[j]) - (1 - core) * pairs
            b = lax.dynamic_slice_in_dim(recv, other_slot * shard_width, shard_width, 1)
            blocks[j] = jnp.where(near[j], a, b)
            blocks[j + pairs] = jnp.where(near[j], b, a)
        return ring.scatter_sum(blocks)

    branch = scattered(jnp.dot(activation, down_weight, preferred_element_type=f32).astype(bf16))
    block_out = (as_float + branch).astype(bf16)

    normed_half = contract(hidden_grad, up_weight, 1, 1)
    product = normed_half * normed_cols.astype(f32)
    first_part = jnp.sum(normed_half * gain_half, axis=1)
    second_part = jnp.sum(product, axis=1)
    gain_part = jnp.sum(product, axis=0)
    by_token = jnp.stack([first_part, second_part]).reshape(2, 2, tok_count)
    by_token = jnp.where(core == 0, by_token, by_token[:, ::-1])
    gain_full = lax.dynamic_update_slice(jnp.zeros((model_width,), f32), gain_part, (core * half_width,))
    small = jnp.concatenate([by_token.reshape(-1), gain_full])
    small = ring.total(small + swap(small))
    by_token = small[: 4 * tok_count].reshape(2, 2, tok_count)
    by_token = lax.dynamic_index_in_dim(by_token, core, 1, keepdims=False) / model_width
    grad_gain = lax.dynamic_slice_in_dim(small, 4 * tok_count + row * shard_width, shard_width, 0) / gain_local

    normed_grad = scattered(normed_half.astype(bf16))
    grad_out = contract(activation, cot_cols, 0, 0).astype(bf16)
    grad_in = contract(normed_cols, hidden_grad, 0, 0).astype(bf16)
    grad_bias = jnp.sum(hidden_grad.astype(f32), axis=0)
    scaled = normed_grad * gain_local
    grad_x = (
        cotangent.astype(f32)
        + inverse_std * (scaled - by_token[0][:, None] - whitened * by_token[1][:, None])
    ).astype(bf16)
    return (block_out, grad_x, grad_in, grad_out, grad_bias, grad_gain)


def local(tokens, cotangent, up_weight, up_bias, down_weight, norm_gain):
    tok_count, shard_width = tokens.shape
    n = lax.axis_size("row")
    if n != ring_limit:
        return wide(tokens, cotangent, up_weight, up_bias, down_weight, norm_gain)
    model_width = n * shard_width
    half_width = model_width // 2
    core = lax.axis_index("col")
    row = lax.axis_index("row")
    other = 1 - core
    ring = Ring(n)
    pairs = n // 2
    mid = tok_count // 2

    rows_near = [ring.row_at(j) for j in range(pairs)]
    rows_far = [ring.row_at(j + pairs) for j in range(pairs)]
    near = [(r // pairs) == core for r in rows_near]
    rows_here = [jnp.where(s, a, b) for s, a, b in zip(near, rows_near, rows_far)]
    near_flags = jnp.stack([s.astype(jnp.int32) for s in near])
    where = jnp.stack([r - core * pairs for r in rows_here] + [core, other] + rows_here).astype(jnp.int32)
    gain_local = lax.dynamic_slice_in_dim(norm_gain, row * shard_width, shard_width, 0)
    gain_half = lax.dynamic_slice_in_dim(norm_gain, core * half_width, half_width, 0)[None]

    def hop(up, down):
        return ring.shift(up, -1), ring.shift(down, 1)

    def crossed(blocks):
        return [swap(jnp.where(near[j], blocks[j + pairs], blocks[j])) for j in range(pairs)]

    t1 = hop(tokens, tokens)
    s0 = shard_stats([tokens])
    t1 = tie(t1, s0)
    t2 = hop(*t1)
    up_near, down_near = up_weight, down_weight
    s1 = shard_stats(t1)
    t2 = tie(t2, s1)
    t3 = hop(*t2)
    s2 = shard_stats(t2)
    t3 = tie(t3, s2)
    t4 = ring.shift(t3[0], -1)
    late = tie([cotangent], [t3[0]])[0]
    c1 = hop(late, late)
    s3 = shard_stats(t3)
    norms = shard_stats([t4], s0 + s1 + s2 + s3)[0]
    t_blocks = [tokens, t1[0], t2[0], t3[0], t4, t3[1], t2[1], t1[1]]
    normed_cols, mark = assemble(t_blocks, crossed(t_blocks), near_flags, where, (norms, swap(norms), gain_half))

    c1 = tie(c1, [norms])
    c2 = hop(*c1)
    hidden_give, mark = side_product(normed_cols, up_near, other, False, True, after=[c1[0]])
    c2 = tie(c2, [mark])
    c3 = hop(*c2)
    hidden_came = swap(tie([hidden_give], [c2[0]])[0])
    hidden_keep, mark = side_product(normed_cols, up_near, core, False, False, after=[c2[0]])
    c3 = tie(c3, [mark])
    c4 = ring.shift(c3[1], 1)
    act_own, act_turned, slope = gelu_half(hidden_keep, hidden_came, up_bias[None], core, after=[c3[0]])
    act_came = swap(act_turned)
    b1, b1_give, mark = branch_pairs(act_own, act_came, down_near, where, 0, shard_width)
    c4 = tie([c4], [mark])[0]
    b1_give = tie([b1_give], [c4])[0]
    c_blocks = [cotangent, c1[0], c2[0], c3[0], c4, c3[1], c2[1], c1[1]]
    c_came = swap(other_half(c_blocks, near_flags))

    branch = Sum(ring, near_flags, [b1, None], [swap(b1_give), None], 0)
    got, _, mark = branch.hop(1, [None, None], after=[mark])
    b2, b2_give, mark = branch_pairs(act_own, act_came, down_near, where, 2, shard_width, after=[mark])
    branch.kept[1], branch.came[1] = b2, swap(tie([b2_give], [got[0]])[0])
    cot_cols, mark = assemble(c_blocks, c_came, near_flags, where, after=[mark])
    got, _, mark = branch.hop(2, got, after=[mark])
    grad_give, mark = side_product(cot_cols, down_near, other, True, True, after=[mark])
    got, _, mark = branch.hop(3, got, after=[mark])
    grad_came = swap(tie([grad_give], [mark])[0])
    grad_keep, mark = side_product(cot_cols, down_near, core, True, False, after=[mark])
    branch_got, _, mark = branch.hop(4, got, after=[mark])
    hid_own, hid_turned, mark = slope_half(grad_keep, grad_came, slope, after=[mark])
    hid_came = swap(hid_turned)
    grad_out, mark = out_grad(act_own, cot_cols, core, 0, None, after=[mark])

    n1, n1_give, small = normed_pairs(
        hid_own, hid_came, up_near, gain_half, normed_cols, where, 0, shard_width, None, after=[mark]
    )
    branch_got = tie(branch_got, [small])
    block_out = (tokens.astype(f32) + branch.last(near[0], branch_got)).astype(bf16)
    n1_give = tie([n1_give], branch_got)[0]
    grad_out, mark = out_grad(act_own, cot_cols, core, 1, grad_out, after=[small])
    norm = Sum(ring, near_flags, [n1, None], [swap(n1_give), None], 1)
    got, _, mark = norm.hop(1, [None, None], after=[mark])
    n2, n2_give, small = normed_pairs(
        hid_own, hid_came, up_near, gain_half, normed_cols, where, 2, shard_width, small, after=[mark]
    )
    n2_give, small = tie([n2_give, small], [got[1]])
    norm.kept[1], norm.came[1] = n2, swap(n2_give)
    small_got = swap(small)
    grad_out, mark = out_grad(act_came, cot_cols, other, 0, grad_out, after=[small])

    def toward(x, step):
        return lax.ppermute(x, "row", [(i, i ^ step) for i in range(n)])

    got, small, mark = norm.hop(2, got, (small, small_got), after=[mark])
    small_got = toward(small, 1)
    grad_in, mark, grad_bias = in_grad(normed_cols, hid_own, hid_came, core, 0, None, after=[mark])
    got, small, mark = norm.hop(3, got, (small, small_got), after=[mark])
    small_got = toward(small, 2)
    grad_in, mark = in_grad(normed_cols, hid_own, hid_came, core, 1, grad_in, after=[mark])
    got, small, mark = norm.hop(4, got, (small, small_got), after=[mark])
    small_got = toward(small, 4)
    grad_out, mark = out_grad(act_came, cot_cols, other, 1, grad_out, after=[mark])
    got = tie(got, [mark])
    small = small + small_got
    token_mean, inverse_std = norms[:, :1], norms[:, 1:]
    by_token = lax.dynamic_index_in_dim(small, n + core, 0, keepdims=False) / model_width
    by_token = [by_token[:tok_count], by_token[256 : 256 + tok_count]]
    grad_gain = lax.dynamic_index_in_dim(small, row, 0, keepdims=False) / gain_local
    scaled = norm.last(near[0], got) * gain_local
    whitened = (tokens.astype(f32) - token_mean) * inverse_std
    grad_x = (
        cotangent.astype(f32)
        + inverse_std * (scaled - by_token[0][:, None] - whitened * by_token[1][:, None])
    ).astype(bf16)
    return (block_out, grad_x, grad_in, grad_out, grad_bias.reshape(-1), grad_gain)


def solution(mesh):
    return jax.shard_map(
        local,
        mesh=mesh,
        in_specs=(
            P(("groups", "col"), "row"),
            P(("groups", "col"), "row"),
            P("col", "row"),
            P("row"),
            P("row", "col"),
            P(),
        ),
        out_specs=(
            P(("groups", "col"), "row"),
            P(("groups", "col"), "row"),
            P(("groups", "col"), "row"),
            P(("groups", "row"), "col"),
            P(("groups", "row")),
            P(("groups", "row")),
        ),
        check_vma=False,
    )
```
